32 devices in a mesh: pp: 2 (over y), ep: 16 (over z, x, core).
Axes of the slice: x: 2, y: 2, z: 4, core: 2. Of those that a mesh axis runs over, the one named last changes fastest.
Arguments:
- fwd_tokens: bfloat16 [2, 2048, 4096], P('pp', 'ep'), may hold values from -6 to 6
- fwd_routes: int32 [2, 2048, 1], P('pp', 'ep'), may hold values from 0 to 3; in each aligned block of 128 rows (0 to 127, 128 to 255, ..., all dimensions but the last counted through in order) at most 48 rows name the same one
- fwd_gates: float32 [2, 2048, 1], P('pp', 'ep'), may hold values from 0.05 to 0.6
- bwd_tokens: bfloat16 [2, 2048, 4096], P('pp', 'ep'), may hold values from -6 to 6
- bwd_grads: bfloat16 [2, 2048, 4096], P('pp', 'ep'), may hold values from -6 to 6
- bwd_routes: int32 [2, 2048, 1], P('pp', 'ep'), may hold values from 0 to 3; in each aligned block of 128 rows (0 to 127, 128 to 255, ..., all dimensions but the last counted through in order) at most 48 rows name the same one
- bwd_gates: float32 [2, 2048, 1], P('pp', 'ep'), may hold values from 0.05 to 0.6
- gate_proj: bfloat16 [2, 16, 1024, 768], P('pp', 'ep'), may hold values from -0.09375 to 0.09375
- up_proj: bfloat16 [2, 16, 1024, 768], P('pp', 'ep'), may hold values from -0.09375 to 0.09375
- down_proj: bfloat16 [2, 16, 768, 1024], P('pp', 'ep'), may hold values from -0.21875 to 0.21875
Outputs:
- handed_forward: bfloat16 [2, 2048, 4096], P('pp', 'ep')
- handed_backward: bfloat16 [2, 2048, 4096], P('pp', 'ep')
The draws below stay inside these ranges and needn't reach their ends.
Inputs may be any that keep to these rules, and one draw needn't show every extreme that they name: `fwd_routes`: among the 128 tokens of one index of ep, no expert is named by more than 48 tokens, and in some such block an expert is named exactly 48 times. `bwd_routes`: among the 128 tokens of one index of ep, no expert is named by more than 48 tokens, and in some such block an expert is named exactly 48 times.
All inputs are finite; a program needn't handle non-finite values.
Results may differ from the reference program's by a relative error of at most 0.0071.
Values may be sent and summed in bfloat16 or wider, within the bound.
No kernel may reach another device: no remote copies, remote signals or barrier semaphores. Data moves between devices by JAX's collectives and lax.ppermute only.
A program may use at most 128 MiB of HBM per device.

```python
import math
import jax
import jax.numpy as jnp
import numpy as np
from jax import lax

D = 4096
FF = 768
TOPW = 1
TD = 128
EXP_WIN = 4
CAP = 48
TOKENS = 2048
N_PP = 2
N_EP = 16


def shard_levels(stream_key, dims, pieces, least, high):
    loudness = 1.0
    for axis_at, shards_of in pieces:
        draws = jax.random.uniform(jax.random.fold_in(jax.random.fold_in(stream_key, 6), axis_at), (shards_of,), jnp.float32, least / len(pieces), high / len(pieces))
        loudness = loudness * jnp.repeat(jnp.exp(draws), dims[axis_at] // shards_of).reshape((-1,) + (1,) * (len(dims) - 1 - axis_at))
    return loudness


def routed_block(rng, own, number, rows, count, top, most, skew):
    ranking = jax.random.permutation(rng, count)
    heavy_load, common = load_shares(count, rows * top, most, skew, True), load_shares(count, rows * top, most, skew, False)
    places = jnp.arange(count)

    def named(lengths, turn):
        used = int((lengths > 0).sum())
        fixed = max(1, used // 4)
        moved = fixed + (places - fixed + turn * (used - fixed)) % max(1, count - fixed)
        return jnp.zeros((count,), jnp.int32).at[ranking[jnp.where(places < fixed, places, moved)]].set(jnp.asarray(lengths, jnp.int32))

    lengths = jnp.where(number % 4 == 0, named(heavy_load, number // 4), named(common, number - number // 4 - 1))
    mixed = jax.random.permutation(jax.random.fold_in(own, 3), count)
    giver, taker = mixed[0:count // 2 * 2:2], mixed[1:count // 2 * 2:2]
    room = jnp.minimum(lengths[giver] - 1, most - lengths[taker]) // 2
    room = jnp.where((giver == ranking[0]) | (taker == ranking[0]) | (lengths[taker] == 0), 0, jnp.maximum(room, 0))
    moved = jax.random.randint(jax.random.fold_in(own, 4), (count // 2,), 0, 1 << 20) % (room + 1)
    lengths = lengths.at[giver].add(-moved).at[taker].add(moved)
    labels = jnp.searchsorted(jnp.cumsum(lengths), jnp.arange(rows * top), side="right").astype(jnp.int32)
    grid = labels.reshape(top, rows).T
    grid = grid[jax.random.permutation(jax.random.fold_in(own, 1), rows)]
    turn = jax.random.randint(jax.random.fold_in(own, 2), (rows, 1), 0, top)
    return jnp.take_along_axis(grid, (jnp.arange(top)[None, :] + turn) % top, axis=1)


def load_shares(count, total, limit, lean, full):
    weights = [(1 << 20) // math.isqrt(grade ** lean) + 1 for grade in range(1, count + 1)]
    largest = limit if full else min(limit, max(-(-total // count), total * weights[0] // sum(weights)))
    least = 1 if total - largest >= count - 1 else 0
    counts, surplus = [largest] + [least] * (count - 1), total - largest - least * (count - 1)
    while surplus > 0:
        candidates = [i for i in range(1, count) if counts[i] < largest] or [i for i in range(1, count) if counts[i] < limit]
        whole, budget = sum([weights[i] for i in candidates]), surplus
        for i in candidates:
            extra = min(limit - counts[i], max(1, budget * weights[i] // whole), surplus)
            counts[i] = counts[i] + extra
            surplus = surplus - extra
    return np.array(counts)


def normal_values(stream_key, shape, width, limit, cuts=(), kind=jnp.bfloat16):
    factor_of = shard_levels(stream_key, shape, cuts, -0.22, 0.18) if cuts else 1.0
    values = jax.random.normal(stream_key, shape, jnp.float32) * width * factor_of
    return jnp.minimum(jnp.maximum(values, -limit), limit).astype(kind)


def setup_inputs(seed: int = 0) -> dict:
    seeds = jax.random.split(jax.random.key(seed), 11)
    fwd_tokens = normal_values(seeds[0], (N_PP, TOKENS, D), 1.0, 6.0, ((0, 2), (1, 16)))
    fwd_routes_keys = jax.random.split(jax.random.fold_in(seeds[1], 1), N_PP * TOKENS // TD)
    fwd_routes_turns = jax.random.permutation(jax.random.fold_in(seeds[1], 3), N_PP * TOKENS // TD)
    fwd_routes = jax.vmap(lambda own, number: routed_block(jax.random.fold_in(seeds[1], 2), own, number, TD, EXP_WIN, TOPW, CAP, 2))(fwd_routes_keys, fwd_routes_turns).reshape((N_PP, TOKENS, TOPW))
    fwd_gates = jnp.clip(jnp.exp(math.log(0.6) - 2.4849067 * jax.random.uniform(seeds[2], (N_PP, TOKENS, TOPW), jnp.float32) ** shard_levels(seeds[2], (N_PP, TOKENS, TOPW), ((0, 2), (1, 16)), -0.2, 0.2)), 0.05, 0.6)
    bwd_tokens = normal_values(seeds[3], (N_PP, TOKENS, D), 1.0, 6.0, ((0, 2), (1, 16)))
    bwd_grads = normal_values(seeds[4], (N_PP, TOKENS, D), 1.0, 6.0, ((0, 2), (1, 16)))
    bwd_routes_keys = jax.random.split(jax.random.fold_in(seeds[5], 1), N_PP * TOKENS // TD)
    bwd_routes_turns = jax.random.permutation(jax.random.fold_in(seeds[5], 3), N_PP * TOKENS // TD)
    bwd_routes = jax.vmap(lambda own, number: routed_block(jax.random.fold_in(seeds[5], 2), own, number, TD, EXP_WIN, TOPW, CAP, 2))(bwd_routes_keys, bwd_routes_turns).reshape((N_PP, TOKENS, TOPW))
    bwd_gates = jnp.clip(jnp.exp(math.log(0.6) - 2.4849067 * jax.random.uniform(seeds[6], (N_PP, TOKENS, TOPW), jnp.float32) ** shard_levels(seeds[6], (N_PP, TOKENS, TOPW), ((0, 2), (1, 16)), -0.2, 0.2)), 0.05, 0.6)
    gate_proj = normal_values(seeds[7], (N_PP, 4 * EXP_WIN, D // 4, FF), D ** -0.5, 0.09375, ((0, 2), (1, 16)))
    up_proj = normal_values(seeds[8], (N_PP, 4 * EXP_WIN, D // 4, FF), D ** -0.5, 0.09375, ((0, 2), (1, 16)))
    down_proj = normal_values(seeds[9], (N_PP, 4 * EXP_WIN, FF, D // 4), FF ** -0.5, 0.21875, ((0, 2), (1, 16)))
    return {"fwd_tokens": fwd_tokens, "fwd_routes": fwd_routes, "fwd_gates": fwd_gates, "bwd_tokens": bwd_tokens, "bwd_grads": bwd_grads, "bwd_routes": bwd_routes, "bwd_gates": bwd_gates, "gate_proj": gate_proj, "up_proj": up_proj, "down_proj": down_proj}


def slot_places(routes):
    flat_routes = routes.reshape(-1)
    onehot = (flat_routes[:, None] == jnp.arange(EXP_WIN, dtype=jnp.int32)[None, :]).astype(jnp.int32)
    before = jnp.cumsum(onehot, axis=0) - onehot
    position = jnp.sum(before * onehot, axis=1)
    slot_match = (position[:, None] == jnp.arange(CAP, dtype=jnp.int32)[None, :]).astype(jnp.float32)
    placed = onehot.astype(jnp.float32)[:, :, None] * slot_match[:, None, :]
    return placed.reshape(TD, TOPW, EXP_WIN, CAP)


def spread_rows(places, values):
    laid_out = values.astype(jnp.float32).reshape(N_EP, TD, 4, D // 4)
    return jnp.einsum("ntkec,nthf->ehncf", places, laid_out)


def device_rows(placed):
    return placed.astype(jnp.bfloat16).reshape(N_EP, N_EP * CAP, D // 4)


def both_partials(row_blocks, gate_mats, up_mats):
    def project_pair(packed):
        block, gate_mat, up_mat = packed
        gate_part = jnp.dot(block, gate_mat, preferred_element_type=jnp.float32)
        up_part = jnp.dot(block, up_mat, preferred_element_type=jnp.float32)
        return jnp.concatenate([gate_part, up_part], axis=1).astype(jnp.bfloat16)

    return lax.map(project_pair, (row_blocks, gate_mats, up_mats))


def quad_total(partials):
    shaped = partials.reshape(EXP_WIN, 4, partials.shape[1], partials.shape[2]).astype(jnp.float32)
    return shaped[:, 0] + shaped[:, 1] + shaped[:, 2] + shaped[:, 3]


def collect(places, returned):
    shaped = returned.reshape(EXP_WIN, 4, N_EP, CAP, D // 4).astype(jnp.float32)
    return jnp.einsum("ntkec,ehncf->ntkhf", places, shaped)


def down_apply(packed):
    hidden_block, down_mat = packed
    return jnp.dot(hidden_block, down_mat, preferred_element_type=jnp.float32).astype(jnp.bfloat16)


def down_back(packed):
    grad_block, down_mat = packed
    return jnp.dot(grad_block, down_mat.T, preferred_element_type=jnp.float32).astype(jnp.bfloat16)


def input_back(packed):
    gate_grad, up_grad, gate_mat, up_mat = packed
    summed = jnp.dot(gate_grad, gate_mat.T, preferred_element_type=jnp.float32)
    summed = summed + jnp.dot(up_grad, up_mat.T, preferred_element_type=jnp.float32)
    return summed.astype(jnp.bfloat16)


def section_step(packed):
    (fwd_x, fwd_r, fwd_g, bwd_x, bwd_dy, bwd_r, bwd_g, gate_mats, up_mats, down_mats) = packed
    places_fwd = jax.vmap(slot_places)(fwd_r.reshape(N_EP, TD, TOPW))
    places_bwd = jax.vmap(slot_places)(bwd_r.reshape(N_EP, TD, TOPW))

    rows_fwd = device_rows(spread_rows(places_fwd, fwd_x))
    sum_fwd = quad_total(both_partials(rows_fwd, gate_mats, up_mats))
    hidden_fwd = (jax.nn.silu(sum_fwd[:, :, :FF]) * sum_fwd[:, :, FF:]).astype(jnp.bfloat16)
    expert_out = lax.map(down_apply, (jnp.repeat(hidden_fwd, 4, axis=0), down_mats))
    gathered = collect(places_fwd, expert_out)
    weights_fwd = fwd_g.reshape(N_EP, TD, TOPW)[:, :, :, None, None]
    mixture = jnp.sum(gathered * weights_fwd, axis=2).reshape(TOKENS, D).astype(jnp.bfloat16)

    slot_gate = jnp.einsum("ntkec,ntk->nec", places_bwd, bwd_g.reshape(N_EP, TD, TOPW))
    slot_scale = jnp.transpose(slot_gate, (1, 0, 2))[:, None, :, :, None]
    rows_bwd = device_rows(spread_rows(places_bwd, bwd_x))
    grads_bwd = device_rows(spread_rows(places_bwd, bwd_dy) * slot_scale)
    sum_bwd = quad_total(both_partials(rows_bwd, gate_mats, up_mats))
    grad_hidden = quad_total(lax.map(down_back, (grads_bwd, down_mats)))
    gate_value = sum_bwd[:, :, :FF]
    up_value = sum_bwd[:, :, FF:]
    sigmoid_value = jax.nn.sigmoid(gate_value)
    grad_gate = (grad_hidden * up_value * sigmoid_value * (1.0 + gate_value * (1.0 - sigmoid_value))).astype(jnp.bfloat16)
    grad_up = (grad_hidden * gate_value * sigmoid_value).astype(jnp.bfloat16)
    grad_rows = lax.map(input_back, (jnp.repeat(grad_gate, 4, axis=0), jnp.repeat(grad_up, 4, axis=0), gate_mats, up_mats))
    grad_input = jnp.sum(collect(places_bwd, grad_rows), axis=2).reshape(TOKENS, D).astype(jnp.bfloat16)
    return mixture, grad_input


def reference(fwd_tokens, fwd_routes, fwd_gates, bwd_tokens, bwd_grads, bwd_routes, bwd_gates, gate_proj, up_proj, down_proj):
    mixture, grad_input = lax.map(section_step, (fwd_tokens, fwd_routes, fwd_gates, bwd_tokens, bwd_grads, bwd_routes, bwd_gates, gate_proj, up_proj, down_proj))
    blank_rows = jnp.zeros((1, TOKENS, D), jnp.bfloat16)
    handed_forward = jnp.concatenate([blank_rows, mixture[:-1]], axis=0)
    handed_backward = jnp.concatenate([grad_input[1:], blank_rows], axis=0)
    return (handed_forward, handed_backward)
```

```python
import functools

import jax
import jax.numpy as jnp
from jax import lax
from jax.experimental import pallas as pl
from jax.experimental.pallas import tpu as pltpu
from jax.sharding import PartitionSpec as P

QUARTERS = 4


def paired(block, distance):
    count = lax.axis_size("ep")
    return lax.ppermute(block, "ep", [(i, i ^ distance) for i in range(count)])


def handed(block, by, distance):
    sections, count = lax.axis_size("pp"), lax.axis_size("ep")
    route = [
        (s * count + i, (s + by) * count + (i ^ distance))
        for s in range(sections)
        if 0 <= s + by < sections
        for i in range(count)
    ]
    return lax.ppermute(block, ("pp", "ep"), route)


def quarters_of(weight):
    across = paired(weight, 2)
    return [weight, paired(weight, 1), across, paired(across, 1)]


def slot_rows(route_row, expert, slot_cap):
    count = route_row.shape[1]
    named = route_row == expert
    low = lax.broadcasted_iota(jnp.int32, (count, count), 0)
    high = lax.broadcasted_iota(jnp.int32, (count, count), 1)
    earlier = jnp.where(low < high, 1.0, 0.0).astype(jnp.bfloat16)
    hits = jnp.broadcast_to(jnp.where(named, 1.0, 0.0), (8, count)).astype(jnp.bfloat16)
    place = jnp.dot(hits, earlier, preferred_element_type=jnp.float32)[:1]
    slots = lax.broadcasted_iota(jnp.int32, (slot_cap, count), 0)
    taken = (slots == place.astype(jnp.int32)) & named
    return jnp.where(taken, 1.0, 0.0).astype(jnp.bfloat16)


def spread_kernel(slot_cap, experts, scaled, where_ref, route_ref, *refs):
    if scaled:
        gate_ref, refs = refs[0], refs[1:]
    value_ref, out_refs = refs[0], refs[1:]
    values = value_ref[...]
    if scaled:
        values = (values.astype(jnp.float32) * gate_ref[...]).astype(jnp.bfloat16)
    for distance in range(experts):
        chosen = slot_rows(route_ref[...], where_ref[0] ^ distance, slot_cap)
        out_refs[distance][...] = jnp.dot(
            chosen, values, preferred_element_type=jnp.float32
        ).astype(jnp.bfloat16)


def spread(where, route_row, values, slot_cap, experts, gates=None):
    tokens, width = values.shape
    quarter = width // QUARTERS
    whole = lambda *shape: pl.BlockSpec(shape, lambda j, where: (0, 0))
    in_specs = [whole(1, tokens)]
    args = [route_row]
    if gates is not None:
        in_specs.append(whole(tokens, 1))
        args.append(gates)
    in_specs.append(pl.BlockSpec((tokens, quarter), lambda j, where: (0, where[1] ^ j)))
    args.append(values)
    return pl.pallas_call(
        functools.partial(spread_kernel, slot_cap, experts, gates is not None),
        grid_spec=pltpu.PrefetchScalarGridSpec(
            num_scalar_prefetch=1,
            grid=(QUARTERS,),
            in_specs=in_specs,
            out_specs=[pl.BlockSpec((slot_cap, quarter), lambda j, where: (0, j))] * experts,
        ),
        out_shape=[jax.ShapeDtypeStruct((slot_cap, width), jnp.bfloat16)] * experts,
        cost_estimate=pl.CostEstimate(
            flops=2 * experts * slot_cap * tokens * width,
            bytes_accessed=2 * width * (tokens + experts * slot_cap),
            transcendentals=0,
        ),
    )(where, *args)


def collect_kernel(slot_cap, experts, scaled, where_ref, route_ref, *refs):
    if scaled:
        gate_ref, refs = refs[0], refs[1:]
    block_refs, out_ref = refs[:-1], refs[-1]
    total = None
    for distance in range(experts):
        chosen = slot_rows(route_ref[...], where_ref[0] ^ distance, slot_cap)
        part = lax.dot_general(
            chosen,
            block_refs[distance][...],
            (((0,), (0,)), ((), ())),
            preferred_element_type=jnp.float32,
        )
        total = part if total is None else total + part
    if scaled:
        total = total * gate_ref[...]
    out_ref[...] = total.astype(jnp.bfloat16)


def collect(where, route_row, blocks, gates=None):
    tokens = route_row.shape[1]
    experts = len(blocks)
    slot_cap, width = blocks[0].shape
    quarter = width // QUARTERS
    whole = lambda *shape: pl.BlockSpec(shape, lambda j, where: (0, 0))
    in_specs = [whole(1, tokens)]
    args = [route_row]
    if gates is not None:
        in_specs.append(whole(tokens, 1))
        args.append(gates)
    in_specs += [pl.BlockSpec((slot_cap, quarter), lambda j, where: (0, j))] * experts
    return pl.pallas_call(
        functools.partial(collect_kernel, slot_cap, experts, gates is not None),
        grid_spec=pltpu.PrefetchScalarGridSpec(
            num_scalar_prefetch=1,
            grid=(QUARTERS,),
            in_specs=in_specs,
            out_specs=pl.BlockSpec((tokens, quarter), lambda j, where: (0, where[1] ^ j)),
        ),
        out_shape=jax.ShapeDtypeStruct((tokens, width), jnp.bfloat16),
        cost_estimate=pl.CostEstimate(
            flops=2 * experts * slot_cap * tokens * width,
            bytes_accessed=2 * width * (tokens + experts * slot_cap),
            transcendentals=0,
        ),
    )(where, *args, *blocks)


def rows_times(rows, mats):
    quarter = mats[0].shape[0]
    total = None
    for j, mat in enumerate(mats):
        part = jnp.dot(
            rows[:, j * quarter : (j + 1) * quarter], mat, preferred_element_type=jnp.float32
        )
        total = part if total is None else total + part
    return total


def contract_cols(left, right):
    return lax.dot_general(
        left, right, (((1,), (1,)), ((), ())), preferred_element_type=jnp.float32
    )


def on_device(
    fwd_tokens,
    fwd_routes,
    fwd_gates,
    bwd_tokens,
    bwd_grads,
    bwd_routes,
    bwd_gates,
    gate_proj,
    up_proj,
    down_proj,
):
    experts = lax.axis_size("ep") // QUARTERS
    tokens = fwd_tokens.shape[1]
    slot_cap = 3 * tokens // (2 * experts)
    me = lax.axis_index("ep")
    where = jnp.stack([me // QUARTERS, me % QUARTERS]).astype(jnp.int32)
    fwd_row = fwd_routes[0].reshape(1, tokens)
    bwd_row = bwd_routes[0].reshape(1, tokens)

    gate_mats = quarters_of(gate_proj[0, 0])
    up_mats = quarters_of(up_proj[0, 0])
    down_mats = quarters_of(down_proj[0, 0])

    def exchanged(blocks):
        return [blocks[0]] + [
            paired(blocks[distance], QUARTERS * distance) for distance in range(1, experts)
        ]

    fwd_blocks = exchanged(spread(where, fwd_row, fwd_tokens[0], slot_cap, experts))
    bwd_blocks = exchanged(spread(where, bwd_row, bwd_tokens[0], slot_cap, experts))
    grad_blocks = exchanged(
        spread(where, bwd_row, bwd_grads[0], slot_cap, experts, gates=bwd_gates[0])
    )

    fwd_meta = handed(
        jnp.concatenate([fwd_row.astype(jnp.float32), fwd_gates[0].reshape(1, tokens)]), 1, 0
    )
    bwd_meta = handed(bwd_row.astype(jnp.float32), -1, 0)

    rows = jnp.concatenate(fwd_blocks)
    gate_value, up_value = rows_times(rows, gate_mats), rows_times(rows, up_mats)
    hidden = (jax.nn.silu(gate_value) * up_value).astype(jnp.bfloat16)
    fwd_out = jnp.concatenate(
        [
            jnp.dot(hidden, mat, preferred_element_type=jnp.float32).astype(jnp.bfloat16)
            for mat in down_mats
        ],
        axis=1,
    )

    rows = jnp.concatenate(bwd_blocks)
    gate_value, up_value = rows_times(rows, gate_mats), rows_times(rows, up_mats)
    grads = jnp.concatenate(grad_blocks)
    quarter = down_mats[0].shape[1]
    grad_hidden = sum(
        contract_cols(grads[:, j * quarter : (j + 1) * quarter], mat)
        for j, mat in enumerate(down_mats)
    )
    sigmoid_value = jax.nn.sigmoid(gate_value)
    grad_gate = (
        grad_hidden * up_value * sigmoid_value * (1.0 + gate_value * (1.0 - sigmoid_value))
    ).astype(jnp.bfloat16)
    grad_up = (grad_hidden * gate_value * sigmoid_value).astype(jnp.bfloat16)
    bwd_out = jnp.concatenate(
        [
            (contract_cols(grad_gate, g) + contract_cols(grad_up, u)).astype(jnp.bfloat16)
            for g, u in zip(gate_mats, up_mats)
        ],
        axis=1,
    )

    def returned(out, by):
        return [
            handed(out[d * slot_cap : (d + 1) * slot_cap], by, QUARTERS * d)
            for d in range(experts)
        ]

    fwd_back = returned(fwd_out, 1)
    bwd_back = returned(bwd_out, -1)
    handed_forward = collect(
        where,
        fwd_meta[:1].astype(jnp.int32),
        fwd_back,
        gates=fwd_meta[1:].reshape(tokens, 1),
    )
    handed_backward = collect(where, bwd_meta.astype(jnp.int32), bwd_back)
    return handed_forward[None], handed_backward[None]


def solution(mesh):
    return jax.shard_map(
        on_device,
        mesh=mesh,
        in_specs=(P("pp", "ep", None),) * 7 + (P("pp", "ep", None, None),) * 3,
        out_specs=(P("pp", "ep", None), P("pp", "ep", None)),
        check_vma=False,
    )
```

```python
import functools

import jax
import jax.numpy as jnp
from jax import lax
from jax.experimental import pallas as pl
from jax.experimental.pallas import tpu as pltpu
from jax.sharding import PartitionSpec as P

QUARTERS = 4


def after(block, *done):
    return lax.optimization_barrier((block, *done))[0] if done else block


def paired(block, distance, *done):
    block = after(block, *done)
    count = lax.axis_size("ep")
    return lax.ppermute(block, "ep", [(i, i ^ distance) for i in range(count)])


def handed(block, steps, distance):
    sections, count = lax.axis_size("pp"), lax.axis_size("ep")
    route = [
        (s * count + i, (s + by) * count + (i ^ distance))
        for s in range(sections)
        for by in steps
        if 0 <= s + by < sections
        for i in range(count)
    ]
    return lax.ppermute(block, ("pp", "ep"), route)


def slot_matrix(route, expert_of, slot_cap, experts):
    count = route.shape[1]
    named = [route == expert_of(distance) for distance in range(experts)]
    hits = [jnp.where(one, 1.0, 0.0) for one in named]
    hits += [jnp.zeros_like(hits[0])] * (-experts % 8)
    low = lax.broadcasted_iota(jnp.int32, (count, count), 0)
    high = lax.broadcasted_iota(jnp.int32, (count, count), 1)
    earlier = jnp.where(low < high, 1.0, 0.0).astype(jnp.bfloat16)
    place = jnp.dot(
        jnp.concatenate(hits).astype(jnp.bfloat16), earlier, preferred_element_type=jnp.float32
    ).astype(jnp.int32)
    slots = lax.broadcasted_iota(jnp.int32, (slot_cap, count), 0)
    return jnp.concatenate(
        [jnp.where((slots == place[d : d + 1]) & named[d], 1.0, 0.0) for d in range(experts)]
    )


def spread_kernel(slot_cap, experts, where_ref, fwd_ref, bwd_ref, gate_ref, *refs):
    value_refs, out_refs = refs[:3], refs[3:]
    quarter = value_refs[0].shape[1] // QUARTERS
    fwd_slots, bwd_slots = [
        slot_matrix(ref[...], lambda d: where_ref[0] ^ d, slot_cap, experts)
        for ref in (fwd_ref, bwd_ref)
    ]
    slot_gate = jnp.sum(bwd_slots * gate_ref[...], axis=1, keepdims=True)
    fwd_slots, bwd_slots = fwd_slots.astype(jnp.bfloat16), bwd_slots.astype(jnp.bfloat16)
    for at, chosen in enumerate((fwd_slots, bwd_slots, bwd_slots)):
        for j in range(QUARTERS):
            start = pl.multiple_of((where_ref[1] ^ j) * quarter, quarter)
            values = value_refs[at][:, pl.ds(start, quarter)]
            rows = jnp.dot(chosen, values, preferred_element_type=jnp.float32)
            if at == 2:
                rows = rows * slot_gate
            for d in range(experts):
                out_refs[at * experts + d][:, j * quarter : (j + 1) * quarter] = rows[
                    d * slot_cap : (d + 1) * slot_cap
                ].astype(jnp.bfloat16)


def spread(where, fwd_routes, bwd_routes, gates, values, slot_cap, experts):
    tokens, width = values[0].shape
    args = [*(row.reshape(1, tokens) for row in (fwd_routes, bwd_routes, gates)), *values]
    out_count = experts * len(values)
    vmem = pl.BlockSpec(memory_space=pltpu.VMEM)
    out = pl.pallas_call(
        functools.partial(spread_kernel, slot_cap, experts),
        in_specs=[pl.BlockSpec(memory_space=pltpu.SMEM)] + [vmem] * len(args),
        out_specs=[vmem] * out_count,
        out_shape=[jax.ShapeDtypeStruct((slot_cap, width), jnp.bfloat16)] * out_count,
        cost_estimate=pl.CostEstimate(
            flops=2 * out_count * slot_cap * tokens * width,
            bytes_accessed=2 * width * (tokens * len(values) + out_count * slot_cap),
            transcendentals=0,
        ),
    )(where, *args)
    return [out[at * experts : (at + 1) * experts] for at in range(len(values))]


def collect_kernel(slot_cap, experts, where_ref, meta_ref, *refs):
    block_refs, out_refs = refs[:experts], refs[experts:]
    tokens = meta_ref.shape[1]
    quarter = out_refs[0].shape[1] // QUARTERS
    low = lax.broadcasted_iota(jnp.int32, (tokens, tokens), 1)
    high = lax.broadcasted_iota(jnp.int32, (tokens, tokens), 0)
    route, gate = [
        jnp.sum(jnp.where(low == high, meta_ref[at : at + 1], 0.0), axis=1, keepdims=True)
        for at in range(2)
    ]
    relative = where_ref[0] ^ lax.broadcasted_iota(jnp.int32, (1, 128), 1)
    hits = jnp.where(route == relative.astype(jnp.float32), 1.0, 0.0)
    earlier = jnp.where(low < high, 1.0, 0.0).astype(jnp.bfloat16)
    place = jnp.dot(earlier, hits.astype(jnp.bfloat16), preferred_element_type=jnp.float32)
    slots = lax.broadcasted_iota(jnp.int32, (tokens, slot_cap), 1).astype(jnp.float32)
    chosen = jnp.concatenate(
        [
            jnp.where((slots == place[:, d : d + 1]) & (hits[:, d : d + 1] > 0.0), 1.0, 0.0)
            for d in range(experts)
        ],
        axis=1,
    ).astype(jnp.bfloat16)
    for j in range(QUARTERS):
        part = slice(j * quarter, (j + 1) * quarter)
        rows = jnp.concatenate([ref[:, part] for ref in block_refs])
        total = jnp.dot(chosen, rows, preferred_element_type=jnp.float32) * gate
        start = pl.multiple_of((where_ref[1] ^ j) * quarter, quarter)
        if len(out_refs) == 1:
            out_refs[0][:, pl.ds(start, quarter)] = total.astype(jnp.bfloat16)
        else:
            first = where_ref[2] == 0
            fwd, bwd = jnp.where(first, 0.0, total), jnp.where(first, total, 0.0)
            out_refs[0][:, pl.ds(start, quarter)] = fwd.astype(jnp.bfloat16)
            out_refs[1][:, pl.ds(start, quarter)] = bwd.astype(jnp.bfloat16)


def collect(where, meta, blocks, outputs):
    tokens = meta.shape[1]
    experts = len(blocks)
    slot_cap, width = blocks[0].shape
    vmem = pl.BlockSpec(memory_space=pltpu.VMEM)
    return pl.pallas_call(
        functools.partial(collect_kernel, slot_cap, experts),
        in_specs=[pl.BlockSpec(memory_space=pltpu.SMEM)] + [vmem] * (1 + experts),
        out_specs=[vmem] * outputs,
        out_shape=[jax.ShapeDtypeStruct((tokens, width), jnp.bfloat16)] * outputs,
        cost_estimate=pl.CostEstimate(
            flops=2 * experts * slot_cap * tokens * width,
            bytes_accessed=2 * width * (tokens * outputs + experts * slot_cap),
            transcendentals=0,
        ),
    )(where, meta, *blocks)


def rows_times(rows, mats):
    quarter = mats[0].shape[0]
    total = None
    for j, mat in enumerate(mats):
        part = jnp.dot(
            rows[:, j * quarter : (j + 1) * quarter], mat, preferred_element_type=jnp.float32
        )
        total = part if total is None else total + part
    return total


def contract_cols(left, right):
    return lax.dot_general(
        left, right, (((1,), (1,)), ((), ())), preferred_element_type=jnp.float32
    )


def on_device(
    fwd_tokens,
    fwd_routes,
    fwd_gates,
    bwd_tokens,
    bwd_grads,
    bwd_routes,
    bwd_gates,
    gate_proj,
    up_proj,
    down_proj,
):
    experts = lax.axis_size("ep") // QUARTERS
    tokens = fwd_tokens.shape[1]
    slot_cap = 3 * tokens // (2 * experts)
    me = lax.axis_index("ep")
    section = lax.axis_index("pp")
    where = jnp.stack([me // QUARTERS, me % QUARTERS, section]).astype(jnp.int32)

    fwd_meta = jnp.concatenate(
        [fwd_routes[0].reshape(1, tokens).astype(jnp.float32), fwd_gates[0].reshape(1, tokens)]
    )
    bwd_meta = bwd_routes[0].reshape(1, tokens).astype(jnp.float32)
    bwd_meta = jnp.concatenate([bwd_meta, jnp.ones_like(bwd_meta)])
    merged = lax.axis_size("pp") == 2
    first = section == 0
    if merged:
        metas = [handed(jnp.where(first, fwd_meta, bwd_meta), (1, -1), 0)]
    else:
        metas = [handed(fwd_meta, (1,), 0), handed(bwd_meta, (-1,), 0)]

    gate, up, down = gate_proj[0, 0], up_proj[0, 0], down_proj[0, 0]
    gate_across = paired(gate, 2)
    up_across = paired(up, 2)
    gate_beside = paired(gate, 1)
    up_beside = paired(up, 1)
    down_beside = paired(down, 1)
    fwd_spread, row_spread, grad_spread = spread(
        after(where, gate_beside),
        fwd_routes[0],
        bwd_routes[0],
        bwd_gates[0],
        (fwd_tokens[0], bwd_tokens[0], bwd_grads[0]),
        slot_cap,
        experts,
    )
    order = sorted(range(1, experts), reverse=True)
    last = order[-1]
    fwd_blocks, bwd_blocks, grad_blocks = {}, {}, {}
    for d in order:
        before = (up_beside, down_beside) if d == last else ()
        fwd_blocks[d] = paired(fwd_spread[d], QUARTERS * d, *before)
    for d in order:
        before = metas if d == last else ()
        bwd_blocks[d] = paired(row_spread[d], QUARTERS * d, fwd_blocks[d], *before)
    down_across = paired(down, 2, gate_across)
    gate_diagonal = paired(gate_across, 1, bwd_blocks[last])
    up_diagonal = paired(up_across, 1, bwd_blocks[last])
    for d in order:
        before = (gate_diagonal, up_diagonal) if d == last else (up_across,)
        grad_blocks[d] = paired(grad_spread[d], QUARTERS * d, bwd_blocks[d], *before)
    down_diagonal = paired(down_across, 1, grad_blocks[last])
    gate_mats = [gate, gate_beside, gate_across, gate_diagonal]
    up_mats = [up, up_beside, up_across, up_diagonal]
    down_mats = [down, down_beside, down_across, down_diagonal]
    fwd_blocks = [fwd_spread[0]] + [fwd_blocks[d] for d in range(1, experts)]
    bwd_blocks = [row_spread[0]] + [bwd_blocks[d] for d in range(1, experts)]
    grad_blocks = [grad_spread[0]] + [grad_blocks[d] for d in range(1, experts)]

    rows = jnp.concatenate(fwd_blocks)
    gate_value, up_value = rows_times(rows, gate_mats), rows_times(rows, up_mats)
    hidden = (jax.nn.silu(gate_value) * up_value).astype(jnp.bfloat16)
    fwd_out = jnp.concatenate(
        [
            jnp.dot(hidden, mat, preferred_element_type=jnp.float32).astype(jnp.bfloat16)
            for mat in down_mats
        ],
        axis=1,
    )

    rows = jnp.concatenate(bwd_blocks)
    gate_value, up_value = rows_times(rows, gate_mats), rows_times(rows, up_mats)
    grads = jnp.concatenate(grad_blocks)
    quarter = down_mats[0].shape[1]
    grad_hidden = sum(
        contract_cols(grads[:, j * quarter : (j + 1) * quarter], mat)
        for j, mat in enumerate(down_mats)
    )
    sigmoid_value = jax.nn.sigmoid(gate_value)
    grad_gate = (
        grad_hidden * up_value * sigmoid_value * (1.0 + gate_value * (1.0 - sigmoid_value))
    ).astype(jnp.bfloat16)
    grad_up = (grad_hidden * gate_value * sigmoid_value).astype(jnp.bfloat16)
    bwd_out = jnp.concatenate(
        [
            (contract_cols(grad_gate, g) + contract_cols(grad_up, u)).astype(jnp.bfloat16)
            for g, u in zip(gate_mats, up_mats)
        ],
        axis=1,
    )

    def returned(out, steps):
        parts = [out[d * slot_cap : (d + 1) * slot_cap] for d in range(experts)]
        back = {d: handed(parts[d], steps, QUARTERS * d) for d in reversed(range(experts))}
        return [back[d] for d in range(experts)]

    if merged:
        back = returned(jnp.where(first, fwd_out, bwd_out), (1, -1))
        handed_forward, handed_backward = collect(where, metas[0], back, 2)
    else:
        (handed_forward,) = collect(where, metas[0], returned(fwd_out, (1,)), 1)
        (handed_backward,) = collect(where, metas[1], returned(bwd_out, (-1,)), 1)
    return handed_forward[None], handed_backward[None]


def solution(mesh):
    return jax.shard_map(
        on_device,
        mesh=mesh,
        in_specs=(P("pp", "ep", None),) * 7 + (P("pp", "ep", None, None),) * 3,
        out_specs=(P("pp", "ep", None), P("pp", "ep", None)),
        check_vma=False,
    )
```

```python
import functools

import jax
import jax.numpy as jnp
from jax import lax
from jax.experimental import pallas as pl
from jax.experimental.pallas import tpu as pltpu
from jax.sharding import PartitionSpec as P

QUARTERS = 4


def after(block, *done):
    return lax.optimization_barrier((block, *done))[0] if done else block


def paired(block, distance, *done):
    block = after(block, *done)
    count = lax.axis_size("ep")
    return lax.ppermute(block, "ep", [(i, i ^ distance) for i in range(count)])


def handed(block, steps, distance):
    sections, count = lax.axis_size("pp"), lax.axis_size("ep")
    route = [
        (s * count + i, (s + by) * count + (i ^ distance))
        for s in range(sections)
        for by in steps
        if 0 <= s + by < sections
        for i in range(count)
    ]
    return lax.ppermute(block, ("pp", "ep"), route)


def slot_matrix(route, expert_of, slot_cap, experts):
    count = route.shape[1]
    named = [route == expert_of(distance) for distance in range(experts)]
    hits = [jnp.where(one, 1.0, 0.0) for one in named]
    hits += [jnp.zeros_like(hits[0])] * (-experts % 8)
    low = lax.broadcasted_iota(jnp.int32, (count, count), 0)
    high = lax.broadcasted_iota(jnp.int32, (count, count), 1)
    earlier = jnp.where(low < high, 1.0, 0.0).astype(jnp.bfloat16)
    place = jnp.dot(
        jnp.concatenate(hits).astype(jnp.bfloat16), earlier, preferred_element_type=jnp.float32
    ).astype(jnp.int32)
    slots = lax.broadcasted_iota(jnp.int32, (slot_cap, count), 0)
    return jnp.concatenate(
        [jnp.where((slots == place[d : d + 1]) & named[d], 1.0, 0.0) for d in range(experts)]
    )


def spread_kernel(slot_cap, experts, where_ref, fwd_ref, bwd_ref, gate_ref, *refs):
    value_refs, out_refs = refs[:3], refs[3:]
    quarter = value_refs[0].shape[1] // QUARTERS
    fwd_slots, bwd_slots = [
        slot_matrix(ref[...], lambda d: where_ref[0] ^ d, slot_cap, experts)
        for ref in (fwd_ref, bwd_ref)
    ]
    slot_gate = jnp.sum(bwd_slots * gate_ref[...], axis=1, keepdims=True)
    fwd_slots, bwd_slots = fwd_slots.astype(jnp.bfloat16), bwd_slots.astype(jnp.bfloat16)
    for at, chosen in enumerate((fwd_slots, bwd_slots, bwd_slots)):
        for j in range(QUARTERS):
            start = pl.multiple_of((where_ref[1] ^ j) * quarter, quarter)
            values = value_refs[at][:, pl.ds(start, quarter)]
            rows = jnp.dot(chosen, values, preferred_element_type=jnp.float32)
            if at == 2:
                rows = rows * slot_gate
            for d in range(experts):
                out_refs[at * experts + d][:, j * quarter : (j + 1) * quarter] = rows[
                    d * slot_cap : (d + 1) * slot_cap
                ].astype(jnp.bfloat16)


def spread(where, fwd_routes, bwd_routes, gates, values, slot_cap, experts):
    tokens, width = values[0].shape
    args = [*(row.reshape(1, tokens) for row in (fwd_routes, bwd_routes, gates)), *values]
    out_count = experts * len(values)
    vmem = pl.BlockSpec(memory_space=pltpu.VMEM)
    out = pl.pallas_call(
        functools.partial(spread_kernel, slot_cap, experts),
        in_specs=[pl.BlockSpec(memory_space=pltpu.SMEM)] + [vmem] * len(args),
        out_specs=[vmem] * out_count,
        out_shape=[jax.ShapeDtypeStruct((slot_cap, width), jnp.bfloat16)] * out_count,
        cost_estimate=pl.CostEstimate(
            flops=2 * out_count * slot_cap * tokens * width,
            bytes_accessed=2 * width * (tokens * len(values) + out_count * slot_cap),
            transcendentals=0,
        ),
        compiler_params=pltpu.CompilerParams(vmem_limit_bytes=20 << 20),
    )(where, *[pltpu.with_memory_space_constraint(arg, pltpu.HBM) for arg in args])
    return [out[at * experts : (at + 1) * experts] for at in range(len(values))]


def collect_kernel(slot_cap, experts, where_ref, meta_ref, *refs):
    block_refs, out_refs = refs[:experts], refs[experts:]
    tokens = meta_ref.shape[1]
    quarter = out_refs[0].shape[1] // QUARTERS
    low = lax.broadcasted_iota(jnp.int32, (tokens, tokens), 1)
    high = lax.broadcasted_iota(jnp.int32, (tokens, tokens), 0)
    route, gate = [
        jnp.sum(jnp.where(low == high, meta_ref[at : at + 1], 0.0), axis=1, keepdims=True)
        for at in range(2)
    ]
    relative = where_ref[0] ^ lax.broadcasted_iota(jnp.int32, (1, 128), 1)
    hits = jnp.where(route == relative.astype(jnp.float32), 1.0, 0.0)
    earlier = jnp.where(low < high, 1.0, 0.0).astype(jnp.bfloat16)
    place = jnp.dot(earlier, hits.astype(jnp.bfloat16), preferred_element_type=jnp.float32)
    slots = lax.broadcasted_iota(jnp.int32, (tokens, slot_cap), 1).astype(jnp.float32)
    chosen = jnp.concatenate(
        [
            jnp.where((slots == place[:, d : d + 1]) & (hits[:, d : d + 1] > 0.0), 1.0, 0.0)
            for d in range(experts)
        ],
        axis=1,
    ).astype(jnp.bfloat16)
    for j in range(QUARTERS):
        part = slice(j * quarter, (j + 1) * quarter)
        rows = jnp.concatenate([ref[:, part] for ref in block_refs])
        total = jnp.dot(chosen, rows, preferred_element_type=jnp.float32) * gate
        start = pl.multiple_of((where_ref[1] ^ j) * quarter, quarter)
        if len(out_refs) == 1:
            out_refs[0][:, pl.ds(start, quarter)] = total.astype(jnp.bfloat16)
        else:
            first = where_ref[2] == 0
            fwd, bwd = jnp.where(first, 0.0, total), jnp.where(first, total, 0.0)
            out_refs[0][:, pl.ds(start, quarter)] = fwd.astype(jnp.bfloat16)
            out_refs[1][:, pl.ds(start, quarter)] = bwd.astype(jnp.bfloat16)


def collect(where, meta, blocks, outputs):
    tokens = meta.shape[1]
    experts = len(blocks)
    slot_cap, width = blocks[0].shape
    vmem = pl.BlockSpec(memory_space=pltpu.VMEM)
    return pl.pallas_call(
        functools.partial(collect_kernel, slot_cap, experts),
        in_specs=[pl.BlockSpec(memory_space=pltpu.SMEM)] + [vmem] * (1 + experts),
        out_specs=[vmem] * outputs,
        out_shape=[jax.ShapeDtypeStruct((tokens, width), jnp.bfloat16)] * outputs,
        cost_estimate=pl.CostEstimate(
            flops=2 * experts * slot_cap * tokens * width,
            bytes_accessed=2 * width * (tokens * outputs + experts * slot_cap),
            transcendentals=0,
        ),
        compiler_params=pltpu.CompilerParams(vmem_limit_bytes=16 << 20),
    )(where, meta, *blocks)


def stage_kernel(*refs):
    count = len(refs) // 2
    arrived = refs[-1]
    copies = [
        pltpu.make_async_copy(refs[at], refs[count + at], arrived.at[at]) for at in range(count)
    ]
    for copy in copies:
        copy.start()
    for copy in copies:
        copy.wait()


def staged(weights):
    count = len(weights)
    return pl.pallas_call(
        stage_kernel,
        in_specs=[pl.BlockSpec(memory_space=pl.ANY)] * count,
        out_specs=[pl.BlockSpec(memory_space=pltpu.VMEM)] * count,
        out_shape=[jax.ShapeDtypeStruct(weight.shape, weight.dtype) for weight in weights],
        scratch_shapes=[pltpu.SemaphoreType.DMA((count,))],
        cost_estimate=pl.CostEstimate(
            flops=0,
            bytes_accessed=sum(2 * weight.size * weight.dtype.itemsize for weight in weights),
            transcendentals=0,
        ),
        compiler_params=pltpu.CompilerParams(vmem_limit_bytes=16 << 20),
    )(*[pltpu.with_memory_space_constraint(weight, pltpu.HBM) for weight in weights])


def rows_times(rows, mats):
    quarter = mats[0].shape[0]
    total = None
    for j, mat in enumerate(mats):
        part = jnp.dot(
            rows[:, j * quarter : (j + 1) * quarter], mat, preferred_element_type=jnp.float32
        )
        total = part if total is None else total + part
    return total


def contract_cols(left, right):
    return lax.dot_general(
        left, right, (((1,), (1,)), ((), ())), preferred_element_type=jnp.float32
    )


def on_device(
    fwd_tokens,
    fwd_routes,
    fwd_gates,
    bwd_tokens,
    bwd_grads,
    bwd_routes,
    bwd_gates,
    gate_proj,
    up_proj,
    down_proj,
):
    experts = lax.axis_size("ep") // QUARTERS
    tokens = fwd_tokens.shape[1]
    slot_cap = 3 * tokens // (2 * experts)
    me = lax.axis_index("ep")
    section = lax.axis_index("pp")
    where = jnp.stack([me // QUARTERS, me % QUARTERS, section]).astype(jnp.int32)

    gate, up, down = gate_proj[0, 0], up_proj[0, 0], down_proj[0, 0]
    gate_across = paired(gate, 2)
    up_across = paired(up, 2)
    gate_beside = paired(gate, 1)
    up_beside = paired(up, 1)
    down_beside = paired(down, 1)
    fwd_spread, row_spread, grad_spread = spread(
        after(where, gate_beside),
        fwd_routes[0],
        bwd_routes[0],
        bwd_gates[0],
        (fwd_tokens[0], bwd_tokens[0], bwd_grads[0]),
        slot_cap,
        experts,
    )
    order = sorted(range(1, experts), reverse=True)
    last = order[-1]
    fwd_blocks, bwd_blocks, grad_blocks = {}, {}, {}
    for d in order:
        before = (up_beside, down_beside) if d == last else ()
        fwd_blocks[d] = paired(fwd_spread[d], QUARTERS * d, *before)
    for d in order:
        bwd_blocks[d] = paired(row_spread[d], QUARTERS * d, fwd_blocks[d])
    down_across = paired(down, 2, gate_across)
    gate_diagonal = paired(gate_across, 1, bwd_blocks[last])
    up_diagonal = paired(up_across, 1, bwd_blocks[last])
    for d in order:
        before = (gate_diagonal, up_diagonal) if d == last else (up_across,)
        grad_blocks[d] = paired(grad_spread[d], QUARTERS * d, bwd_blocks[d], *before)
    down_diagonal = paired(down_across, 1, up_diagonal)
    near = lax.optimization_barrier((gate_across, down_beside, fwd_blocks[last]))
    gate_across, down_beside = staged(near[:2])
    near = lax.optimization_barrier((up_across, bwd_blocks[last]))
    (up_across,) = staged(near[:1])
    gate_mats = [gate, gate_beside, gate_across, gate_diagonal]
    up_mats = [up, up_beside, up_across, up_diagonal]
    down_mats = [down, down_beside, down_across, down_diagonal]
    fwd_blocks = [fwd_spread[0]] + [fwd_blocks[d] for d in range(1, experts)]
    bwd_blocks = [row_spread[0]] + [bwd_blocks[d] for d in range(1, experts)]
    grad_blocks = [grad_spread[0]] + [grad_blocks[d] for d in range(1, experts)]

    rows = jnp.concatenate(fwd_blocks)
    gate_value, up_value = rows_times(rows, gate_mats), rows_times(rows, up_mats)
    hidden = (jax.nn.silu(gate_value) * up_value).astype(jnp.bfloat16)
    fwd_parts = [
        jnp.dot(hidden, mat, preferred_element_type=jnp.float32).astype(jnp.bfloat16)
        for mat in down_mats
    ]

    rows = jnp.concatenate(bwd_blocks)
    gate_value, up_value = rows_times(rows, gate_mats), rows_times(rows, up_mats)
    sigmoid_value = jax.nn.sigmoid(gate_value)
    gate_factor = up_value * sigmoid_value * (1.0 + gate_value * (1.0 - sigmoid_value))
    up_factor = gate_value * sigmoid_value

    landed = lax.optimization_barrier((*grad_blocks[1:], gate_factor, up_factor, *fwd_parts))
    grads = jnp.concatenate([grad_blocks[0], *landed[: experts - 1]])
    quarter = down.shape[1]
    grad_hidden = sum(
        contract_cols(grads[:, j * quarter : (j + 1) * quarter], mat)
        for j, mat in enumerate(down_mats)
    )
    grad_gate = (grad_hidden * landed[experts - 1]).astype(jnp.bfloat16)
    grad_up = (grad_hidden * landed[experts]).astype(jnp.bfloat16)
    bwd_parts = [
        (contract_cols(grad_gate, g) + contract_cols(grad_up, u)).astype(jnp.bfloat16)
        for g, u in zip(gate_mats, up_mats)
    ]
    fwd_parts = landed[experts + 1 :]
    merged = lax.axis_size("pp") == 2

    done = tuple(grad_blocks[1:])
    fwd_meta = jnp.concatenate(
        [fwd_routes[0].reshape(1, tokens).astype(jnp.float32), fwd_gates[0].reshape(1, tokens)]
    )
    bwd_meta = bwd_routes[0].reshape(1, tokens).astype(jnp.float32)
    bwd_meta = jnp.concatenate([bwd_meta, jnp.ones_like(bwd_meta)])

    def returned(parts, steps):
        out = jnp.concatenate(parts, axis=1)
        blocks = [out[d * slot_cap : (d + 1) * slot_cap] for d in range(experts)]
        return [handed(blocks[d], steps, QUARTERS * d) for d in range(experts)]

    if merged:
        first = section == 0
        meta = handed(after(jnp.where(first, fwd_meta, bwd_meta), *done), (1, -1), 0)
        parts = [jnp.where(first, fwd, bwd) for fwd, bwd in zip(fwd_parts, bwd_parts)]
        handed_forward, handed_backward = collect(where, meta, returned(parts, (1, -1)), 2)
    else:
        metas = [handed(after(m, *done), (by,), 0) for m, by in ((fwd_meta, 1), (bwd_meta, -1))]
        (handed_forward,) = collect(where, metas[0], returned(fwd_parts, (1,)), 1)
        (handed_backward,) = collect(where, metas[1], returned(bwd_parts, (-1,)), 1)
    return handed_forward[None], handed_backward[None]


def solution(mesh):
    return jax.shard_map(
        on_device,
        mesh=mesh,
        in_specs=(P("pp", "ep", None),) * 7 + (P("pp", "ep", None, None),) * 3,
        out_specs=(P("pp", "ep", None), P("pp", "ep", None)),
        check_vma=False,
    )
```

```python
import functools

import jax
import jax.numpy as jnp
from jax import lax
from jax.experimental import pallas as pl
from jax.experimental.pallas import tpu as pltpu
from jax.sharding import PartitionSpec as P

QUARTERS = 4


def is_inner(place):
    return (place ^ (place >> 1)) & 1


def sent_distances(experts):
    if experts == 4:
        return ((0, 0), (2, 1), (1, 2), (3, 3))
    return tuple((d, d) for d in range(experts))


def handed_distances(experts):
    if experts == 4:
        return ((3, 0), (2, 1), (1, 2), (0, 3))
    return tuple((d, d) for d in range(experts))


def landed_distances(experts):
    if experts == 4:
        return ((3, 0), (1, 2), (2, 1), (0, 3))
    return tuple((d, d) for d in range(experts))


def expert_at(where_ref, distance):
    outer, inner = distance
    return where_ref[0] ^ (outer + where_ref[3] * (inner - outer))


def target(index, distance):
    return index ^ (QUARTERS * distance[is_inner(index // QUARTERS)])


def after(block, *done):
    return lax.optimization_barrier((block, *done))[0] if done else block


def paired(block, distance, *done):
    block = after(block, *done)
    count = lax.axis_size("ep")
    return lax.ppermute(block, "ep", [(i, i ^ distance) for i in range(count)])


def sent(block, distance, *done):
    block = after(block, *done)
    count = lax.axis_size("ep")
    return lax.ppermute(block, "ep", [(i, target(i, distance)) for i in range(count)])


def handed(block, steps, distance):
    sections, count = lax.axis_size("pp"), lax.axis_size("ep")
    route = [
        (s * count + i, (s + by) * count + target(i, distance))
        for s in range(sections)
        for by in steps
        if 0 <= s + by < sections
        for i in range(count)
    ]
    return lax.ppermute(block, ("pp", "ep"), route)


def slot_matrix(route, expert_of, slot_cap, experts):
    count = route.shape[1]
    named = [route == expert_of(distance) for distance in range(experts)]
    hits = [jnp.where(one, 1.0, 0.0) for one in named]
    hits += [jnp.zeros_like(hits[0])] * (-experts % 8)
    low = lax.broadcasted_iota(jnp.int32, (count, count), 0)
    high = lax.broadcasted_iota(jnp.int32, (count, count), 1)
    earlier = jnp.where(low < high, 1.0, 0.0).astype(jnp.bfloat16)
    place = jnp.dot(
        jnp.concatenate(hits).astype(jnp.bfloat16), earlier, preferred_element_type=jnp.float32
    ).astype(jnp.int32)
    slots = lax.broadcasted_iota(jnp.int32, (slot_cap, count), 0)
    return jnp.concatenate(
        [jnp.where((slots == place[d : d + 1]) & named[d], 1.0, 0.0) for d in range(experts)]
    )


def spread_kernel(slot_cap, experts, where_ref, fwd_ref, bwd_ref, gate_ref, *refs):
    value_refs, out_refs = refs[:3], refs[3:]
    quarter = value_refs[0].shape[1] // QUARTERS
    fwd_slots, bwd_slots = [
        slot_matrix(ref[...], lambda d: expert_at(where_ref, sent_distances(experts)[d]), slot_cap, experts)
        for ref in (fwd_ref, bwd_ref)
    ]
    slot_gate = jnp.sum(bwd_slots * gate_ref[...], axis=1, keepdims=True)
    fwd_slots, bwd_slots = fwd_slots.astype(jnp.bfloat16), bwd_slots.astype(jnp.bfloat16)
    for at, chosen in enumerate((fwd_slots, bwd_slots, bwd_slots)):
        for j in range(QUARTERS):
            start = pl.multiple_of((where_ref[1] ^ j) * quarter, quarter)
            values = value_refs[at][:, pl.ds(start, quarter)]
            rows = jnp.dot(chosen, values, preferred_element_type=jnp.float32)
            if at == 2:
                rows = rows * slot_gate
            for d in range(experts):
                out_refs[at * experts + d][:, j * quarter : (j + 1) * quarter] = rows[
                    d * slot_cap : (d + 1) * slot_cap
                ].astype(jnp.bfloat16)


def spread(where, fwd_routes, bwd_routes, gates, values, slot_cap, experts):
    tokens, width = values[0].shape
    args = [*(row.reshape(1, tokens) for row in (fwd_routes, bwd_routes, gates)), *values]
    out_count = experts * len(values)
    vmem = pl.BlockSpec(memory_space=pltpu.VMEM)
    out = pl.pallas_call(
        functools.partial(spread_kernel, slot_cap, experts),
        in_specs=[pl.BlockSpec(memory_space=pltpu.SMEM)] + [vmem] * len(args),
        out_specs=[vmem] * out_count,
        out_shape=[jax.ShapeDtypeStruct((slot_cap, width), jnp.bfloat16)] * out_count,
        cost_estimate=pl.CostEstimate(
            flops=2 * out_count * slot_cap * tokens * width,
            bytes_accessed=2 * width * (tokens * len(values) + out_count * slot_cap),
            transcendentals=0,
        ),
        compiler_params=pltpu.CompilerParams(vmem_limit_bytes=20 << 20),
    )(where, *[pltpu.with_memory_space_constraint(arg, pltpu.HBM) for arg in args])
    return [out[at * experts : (at + 1) * experts] for at in range(len(values))]


def collect_kernel(slot_cap, experts, where_ref, meta_ref, *refs):
    block_refs, out_refs = refs[:experts], refs[experts:]
    tokens = meta_ref.shape[1]
    quarter = out_refs[0].shape[1] // QUARTERS
    low = lax.broadcasted_iota(jnp.int32, (tokens, tokens), 1)
    high = lax.broadcasted_iota(jnp.int32, (tokens, tokens), 0)
    route, gate = [
        jnp.sum(jnp.where(low == high, meta_ref[at : at + 1], 0.0), axis=1, keepdims=True)
        for at in range(2)
    ]
    lane = lax.broadcasted_iota(jnp.int32, (1, 128), 1)
    relative = jnp.full((1, 128), -1, jnp.int32)
    for d, distance in enumerate(landed_distances(experts)):
        relative = jnp.where(lane == d, expert_at(where_ref, distance), relative)
    hits = jnp.where(route == relative.astype(jnp.float32), 1.0, 0.0)
    earlier = jnp.where(low < high, 1.0, 0.0).astype(jnp.bfloat16)
    place = jnp.dot(earlier, hits.astype(jnp.bfloat16), preferred_element_type=jnp.float32)
    slots = lax.broadcasted_iota(jnp.int32, (tokens, slot_cap), 1).astype(jnp.float32)
    chosen = jnp.concatenate(
        [
            jnp.where((slots == place[:, d : d + 1]) & (hits[:, d : d + 1] > 0.0), 1.0, 0.0)
            for d in range(experts)
        ],
        axis=1,
    ).astype(jnp.bfloat16)
    for j in range(QUARTERS):
        part = slice(j * quarter, (j + 1) * quarter)
        rows = jnp.concatenate([ref[:, part] for ref in block_refs])
        total = jnp.dot(chosen, rows, preferred_element_type=jnp.float32) * gate
        start = pl.multiple_of((where_ref[1] ^ j) * quarter, quarter)
        if len(out_refs) == 1:
            out_refs[0][:, pl.ds(start, quarter)] = total.astype(jnp.bfloat16)
        else:
            first = where_ref[2] == 0
            fwd, bwd = jnp.where(first, 0.0, total), jnp.where(first, total, 0.0)
            out_refs[0][:, pl.ds(start, quarter)] = fwd.astype(jnp.bfloat16)
            out_refs[1][:, pl.ds(start, quarter)] = bwd.astype(jnp.bfloat16)


def collect(where, meta, blocks, outputs):
    tokens = meta.shape[1]
    experts = len(blocks)
    slot_cap, width = blocks[0].shape
    vmem = pl.BlockSpec(memory_space=pltpu.VMEM)
    return pl.pallas_call(
        functools.partial(collect_kernel, slot_cap, experts),
        in_specs=[pl.BlockSpec(memory_space=pltpu.SMEM)] + [vmem] * (1 + experts),
        out_specs=[vmem] * outputs,
        out_shape=[jax.ShapeDtypeStruct((tokens, width), jnp.bfloat16)] * outputs,
        cost_estimate=pl.CostEstimate(
            flops=2 * experts * slot_cap * tokens * width,
            bytes_accessed=2 * width * (tokens * outputs + experts * slot_cap),
            transcendentals=0,
        ),
        compiler_params=pltpu.CompilerParams(vmem_limit_bytes=16 << 20),
    )(where, meta, *blocks)


def stage_kernel(*refs):
    count = len(refs) // 2
    arrived = refs[-1]
    copies = [
        pltpu.make_async_copy(refs[at], refs[count + at], arrived.at[at]) for at in range(count)
    ]
    for copy in copies:
        copy.start()
    for copy in copies:
        copy.wait()


def staged(weights):
    count = len(weights)
    return pl.pallas_call(
        stage_kernel,
        in_specs=[pl.BlockSpec(memory_space=pl.ANY)] * count,
        out_specs=[pl.BlockSpec(memory_space=pltpu.VMEM)] * count,
        out_shape=[jax.ShapeDtypeStruct(weight.shape, weight.dtype) for weight in weights],
        scratch_shapes=[pltpu.SemaphoreType.DMA((count,))],
        cost_estimate=pl.CostEstimate(
            flops=0,
            bytes_accessed=sum(2 * weight.size * weight.dtype.itemsize for weight in weights),
            transcendentals=0,
        ),
        compiler_params=pltpu.CompilerParams(vmem_limit_bytes=16 << 20),
    )(*[pltpu.with_memory_space_constraint(weight, pltpu.HBM) for weight in weights])


def rows_times(rows, mats):
    quarter = mats[0].shape[0]
    total = None
    for j, mat in enumerate(mats):
        part = jnp.dot(
            rows[:, j * quarter : (j + 1) * quarter], mat, preferred_element_type=jnp.float32
        )
        total = part if total is None else total + part
    return total


def contract_cols(left, right):
    return lax.dot_general(
        left, right, (((1,), (1,)), ((), ())), preferred_element_type=jnp.float32
    )


def on_device(
    fwd_tokens,
    fwd_routes,
    fwd_gates,
    bwd_tokens,
    bwd_grads,
    bwd_routes,
    bwd_gates,
    gate_proj,
    up_proj,
    down_proj,
):
    experts = lax.axis_size("ep") // QUARTERS
    tokens = fwd_tokens.shape[1]
    slot_cap = 3 * tokens // (2 * experts)
    me = lax.axis_index("ep")
    section = lax.axis_index("pp")
    place = me // QUARTERS
    inner = is_inner(place) if experts == 4 else jnp.zeros_like(place)
    where = jnp.stack([place, me % QUARTERS, section, inner]).astype(jnp.int32)

    gate, up, down = gate_proj[0, 0], up_proj[0, 0], down_proj[0, 0]
    gate_across = paired(gate, 2)
    up_across = paired(up, 2)
    gate_beside = paired(gate, 1)
    up_beside = paired(up, 1)
    down_beside = paired(down, 1)
    fwd_spread, row_spread, grad_spread = spread(
        after(where, gate_beside),
        fwd_routes[0],
        bwd_routes[0],
        bwd_gates[0],
        (fwd_tokens[0], bwd_tokens[0], bwd_grads[0]),
        slot_cap,
        experts,
    )
    order = sorted(range(1, experts), reverse=True)
    distances = sent_distances(experts)
    last = order[-1]
    fwd_blocks, bwd_blocks, grad_blocks = {}, {}, {}
    for d in order:
        before = (up_beside, down_beside) if d == last else ()
        fwd_blocks[d] = sent(fwd_spread[d], distances[d], *before)
    for d in order:
        bwd_blocks[d] = sent(row_spread[d], distances[d], fwd_blocks[d])
    down_across = paired(down, 2, gate_across)
    gate_diagonal = paired(gate_across, 1, bwd_blocks[last])
    up_diagonal = paired(up_across, 1, bwd_blocks[last])
    near = lax.optimization_barrier((gate_across, down_beside, fwd_blocks[last]))
    gate_across, down_beside = staged(near[:2])
    near = lax.optimization_barrier((up_across, bwd_blocks[last]))
    (up_across,) = staged(near[:1])
    gate_mats = [gate, gate_beside, gate_across, gate_diagonal]
    up_mats = [up, up_beside, up_across, up_diagonal]
    fwd_blocks = [fwd_spread[0]] + [fwd_blocks[d] for d in range(1, experts)]

    rows = jnp.concatenate(fwd_blocks)
    gate_value, up_value = rows_times(rows, gate_mats), rows_times(rows, up_mats)
    hidden = (jax.nn.silu(gate_value) * up_value).astype(jnp.bfloat16)
    for d in order:
        before = () if d == last else (hidden,) if d == order[0] else ()
        grad_blocks[d] = sent(grad_spread[d], distances[d], bwd_blocks[d], *before)
    bwd_blocks = [row_spread[0]] + [bwd_blocks[d] for d in range(1, experts)]
    grad_blocks = [grad_spread[0]] + [grad_blocks[d] for d in range(1, experts)]
    rows = jnp.concatenate(lax.optimization_barrier((*bwd_blocks, hidden))[:experts])
    gate_value, up_value = rows_times(rows, gate_mats), rows_times(rows, up_mats)
    sigmoid_value = jax.nn.sigmoid(gate_value)
    gate_factor = up_value * sigmoid_value * (1.0 + gate_value * (1.0 - sigmoid_value))
    up_factor = gate_value * sigmoid_value

    near_parts = [
        jnp.dot(hidden, mat, preferred_element_type=jnp.float32).astype(jnp.bfloat16)
        for mat in (down, down_beside)
    ]
    landed = lax.optimization_barrier((*grad_blocks[1:], gate_factor, up_factor, *near_parts))
    down_across = after(down_across, landed[0])
    down_mats = [down, down_beside, down_across, paired(down_across, 1)]
    grads = jnp.concatenate([grad_blocks[0], *landed[: experts - 1]])
    quarter = down.shape[1]
    grad_hidden = sum(
        contract_cols(grads[:, j * quarter : (j + 1) * quarter], mat)
        for j, mat in enumerate(down_mats)
    )
    grad_gate = (grad_hidden * landed[experts - 1]).astype(jnp.bfloat16)
    grad_up = (grad_hidden * landed[experts]).astype(jnp.bfloat16)
    bwd_parts = [
        (contract_cols(grad_gate, g) + contract_cols(grad_up, u)).astype(jnp.bfloat16)
        for g, u in zip(gate_mats, up_mats)
    ]
    far_parts = [
        jnp.dot(hidden, mat, preferred_element_type=jnp.float32).astype(jnp.bfloat16)
        for mat in down_mats[2:]
    ]
    fwd_parts = [*landed[experts + 1 :], *far_parts]
    merged = lax.axis_size("pp") == 2

    done = tuple(grad_blocks[1:])
    fwd_meta = jnp.concatenate(
        [fwd_routes[0].reshape(1, tokens).astype(jnp.float32), fwd_gates[0].reshape(1, tokens)]
    )
    bwd_meta = bwd_routes[0].reshape(1, tokens).astype(jnp.float32)
    bwd_meta = jnp.concatenate([bwd_meta, jnp.ones_like(bwd_meta)])

    def returned(parts, steps):
        out = jnp.concatenate(parts, axis=1)
        blocks = [out[d * slot_cap : (d + 1) * slot_cap] for d in range(experts)]
        if experts == 4:
            edge = jnp.where(inner == 1, blocks[0], blocks[3])
            core = jnp.where(inner == 1, blocks[3], blocks[0])
            blocks = [edge, blocks[2], blocks[1], core]
        return [handed(b, steps, d) for b, d in zip(blocks, handed_distances(experts))]

    if merged:
        first = section == 0
        meta = handed(after(jnp.where(first, fwd_meta, bwd_meta), *done), (1, -1), (0, 0))
        parts = [jnp.where(first, fwd, bwd) for fwd, bwd in zip(fwd_parts, bwd_parts)]
        handed_forward, handed_backward = collect(where, meta, returned(parts, (1, -1)), 2)
    else:
        metas = [handed(after(m, *done), (by,), (0, 0)) for m, by in ((fwd_meta, 1), (bwd_meta, -1))]
        (handed_forward,) = collect(where, metas[0], returned(fwd_parts, (1,)), 1)
        (handed_backward,) = collect(where, metas[1], returned(bwd_parts, (-1,)), 1)
    return handed_forward[None], handed_backward[None]


def solution(mesh):
    return jax.shard_map(
        on_device,
        mesh=mesh,
        in_specs=(P("pp", "ep", None),) * 7 + (P("pp", "ep", None, None),) * 3,
        out_specs=(P("pp", "ep", None), P("pp", "ep", None)),
        check_vma=False,
    )
```

```python
import functools

import jax
import jax.numpy as jnp
from jax import lax
from jax.experimental import pallas as pl
from jax.experimental.pallas import tpu as pltpu
from jax.sharding import PartitionSpec as P

QUARTERS = 4


def is_inner(place):
    return (place ^ (place >> 1)) & 1


def sent_distances(experts):
    if experts == 4:
        return ((0, 0), (2, 1), (1, 2), (3, 3))
    return tuple((d, d) for d in range(experts))


def handed_distances(experts):
    if experts == 4:
        return ((3, 0), (2, 1), (1, 2), (0, 3))
    return tuple((d, d) for d in range(experts))


def landed_distances(experts):
    if experts == 4:
        return ((3, 0), (1, 2), (2, 1), (0, 3))
    return tuple((d, d) for d in range(experts))


def expert_at(where_ref, distance):
    outer, inner = distance
    return where_ref[0] ^ (outer + where_ref[3] * (inner - outer))


def target(index, distance):
    return index ^ (QUARTERS * distance[is_inner(index // QUARTERS)])


def after(block, *done):
    return lax.optimization_barrier((block, *done))[0] if done else block


def paired(block, distance, *done):
    block = after(block, *done)
    count = lax.axis_size("ep")
    return lax.ppermute(block, "ep", [(i, i ^ distance) for i in range(count)])


def sent(block, distance, *done):
    block = after(block, *done)
    count = lax.axis_size("ep")
    return lax.ppermute(block, "ep", [(i, target(i, distance)) for i in range(count)])


def handed(block, steps, distance):
    sections, count = lax.axis_size("pp"), lax.axis_size("ep")
    route = [
        (s * count + i, (s + by) * count + target(i, distance))
        for s in range(sections)
        for by in steps
        if 0 <= s + by < sections
        for i in range(count)
    ]
    return lax.ppermute(block, ("pp", "ep"), route)


def slot_matrix(route, expert_of, slot_cap, experts):
    count = route.shape[1]
    named = [route == expert_of(distance) for distance in range(experts)]
    hits = [jnp.where(one, 1.0, 0.0) for one in named]
    hits += [jnp.zeros_like(hits[0])] * (-experts % 8)
    low = lax.broadcasted_iota(jnp.int32, (count, count), 0)
    high = lax.broadcasted_iota(jnp.int32, (count, count), 1)
    earlier = jnp.where(low < high, 1.0, 0.0).astype(jnp.bfloat16)
    place = jnp.dot(
        jnp.concatenate(hits).astype(jnp.bfloat16), earlier, preferred_element_type=jnp.float32
    ).astype(jnp.int32)
    slots = lax.broadcasted_iota(jnp.int32, (slot_cap, count), 0)
    return jnp.concatenate(
        [jnp.where((slots == place[d : d + 1]) & named[d], 1.0, 0.0) for d in range(experts)]
    )


def spread_kernel(slot_cap, experts, where_ref, fwd_ref, bwd_ref, gate_ref, *refs):
    value_refs, out_refs = refs[:3], refs[3:]
    quarter = value_refs[0].shape[1] // QUARTERS
    fwd_slots, bwd_slots = [
        slot_matrix(ref[...], lambda d: expert_at(where_ref, sent_distances(experts)[d]), slot_cap, experts)
        for ref in (fwd_ref, bwd_ref)
    ]
    slot_gate = jnp.sum(bwd_slots * gate_ref[...], axis=1, keepdims=True)
    fwd_slots, bwd_slots = fwd_slots.astype(jnp.bfloat16), bwd_slots.astype(jnp.bfloat16)
    for at, chosen in enumerate((fwd_slots, bwd_slots, bwd_slots)):
        for j in range(QUARTERS):
            start = pl.multiple_of((where_ref[1] ^ j) * quarter, quarter)
            values = value_refs[at][:, pl.ds(start, quarter)]
            rows = jnp.dot(chosen, values, preferred_element_type=jnp.float32)
            if at == 2:
                rows = rows * slot_gate
            for d in range(experts):
                out_refs[at * experts + d][:, j * quarter : (j + 1) * quarter] = rows[
                    d * slot_cap : (d + 1) * slot_cap
                ].astype(jnp.bfloat16)


def spread(where, fwd_routes, bwd_routes, gates, values, slot_cap, experts):
    tokens, width = values[0].shape
    args = [*(row.reshape(1, tokens) for row in (fwd_routes, bwd_routes, gates)), *values]
    out_count = experts * len(values)
    vmem = pl.BlockSpec(memory_space=pltpu.VMEM)
    out = pl.pallas_call(
        functools.partial(spread_kernel, slot_cap, experts),
        in_specs=[pl.BlockSpec(memory_space=pltpu.SMEM)] + [vmem] * len(args),
        out_specs=[vmem] * out_count,
        out_shape=[jax.ShapeDtypeStruct((slot_cap, width), jnp.bfloat16)] * out_count,
        cost_estimate=pl.CostEstimate(
            flops=2 * out_count * slot_cap * tokens * width,
            bytes_accessed=2 * width * (tokens * len(values) + out_count * slot_cap),
            transcendentals=0,
        ),
        compiler_params=pltpu.CompilerParams(vmem_limit_bytes=20 << 20),
    )(where, *[pltpu.with_memory_space_constraint(arg, pltpu.HBM) for arg in args])
    return [out[at * experts : (at + 1) * experts] for at in range(len(values))]


def collect_kernel(slot_cap, experts, where_ref, meta_ref, *refs):
    block_refs, out_refs = refs[:experts], refs[experts:]
    tokens = meta_ref.shape[1]
    quarter = out_refs[0].shape[1] // QUARTERS
    low = lax.broadcasted_iota(jnp.int32, (tokens, tokens), 1)
    high = lax.broadcasted_iota(jnp.int32, (tokens, tokens), 0)
    route, gate = [
        jnp.sum(jnp.where(low == high, meta_ref[at : at + 1], 0.0), axis=1, keepdims=True)
        for at in range(2)
    ]
    lane = lax.broadcasted_iota(jnp.int32, (1, 128), 1)
    relative = jnp.full((1, 128), -1, jnp.int32)
    for d, distance in enumerate(landed_distances(experts)):
        relative = jnp.where(lane == d, expert_at(where_ref, distance), relative)
    hits = jnp.where(route == relative.astype(jnp.float32), 1.0, 0.0)
    earlier = jnp.where(low < high, 1.0, 0.0).astype(jnp.bfloat16)
    place = jnp.dot(earlier, hits.astype(jnp.bfloat16), preferred_element_type=jnp.float32)
    slots = lax.broadcasted_iota(jnp.int32, (tokens, slot_cap), 1).astype(jnp.float32)
    chosen = jnp.concatenate(
        [
            jnp.where((slots == place[:, d : d + 1]) & (hits[:, d : d + 1] > 0.0), 1.0, 0.0)
            for d in range(experts)
        ],
        axis=1,
    ).astype(jnp.bfloat16)
    for j in range(QUARTERS):
        part = slice(j * quarter, (j + 1) * quarter)
        rows = jnp.concatenate([ref[:, part] for ref in block_refs])
        total = jnp.dot(chosen, rows, preferred_element_type=jnp.float32) * gate
        start = pl.multiple_of((where_ref[1] ^ j) * quarter, quarter)
        if len(out_refs) == 1:
            out_refs[0][:, pl.ds(start, quarter)] = total.astype(jnp.bfloat16)
        else:
            first = where_ref[2] == 0
            fwd, bwd = jnp.where(first, 0.0, total), jnp.where(first, total, 0.0)
            out_refs[0][:, pl.ds(start, quarter)] = fwd.astype(jnp.bfloat16)
            out_refs[1][:, pl.ds(start, quarter)] = bwd.astype(jnp.bfloat16)


def collect(where, meta, blocks, outputs):
    tokens = meta.shape[1]
    experts = len(blocks)
    slot_cap, width = blocks[0].shape
    vmem = pl.BlockSpec(memory_space=pltpu.VMEM)
    return pl.pallas_call(
        functools.partial(collect_kernel, slot_cap, experts),
        in_specs=[pl.BlockSpec(memory_space=pltpu.SMEM)] + [vmem] * (1 + experts),
        out_specs=[vmem] * outputs,
        out_shape=[jax.ShapeDtypeStruct((tokens, width), jnp.bfloat16)] * outputs,
        cost_estimate=pl.CostEstimate(
            flops=2 * experts * slot_cap * tokens * width,
            bytes_accessed=2 * width * (tokens * outputs + experts * slot_cap),
            transcendentals=0,
        ),
        compiler_params=pltpu.CompilerParams(vmem_limit_bytes=16 << 20),
    )(where, meta, *blocks)


def stage_kernel(*refs):
    count = len(refs) // 2
    arrived = refs[-1]
    copies = [
        pltpu.make_async_copy(refs[at], refs[count + at], arrived.at[at]) for at in range(count)
    ]
    for copy in copies:
        copy.start()
    for copy in copies:
        copy.wait()


def staged(weights):
    count = len(weights)
    return pl.pallas_call(
        stage_kernel,
        in_specs=[pl.BlockSpec(memory_space=pl.ANY)] * count,
        out_specs=[pl.BlockSpec(memory_space=pltpu.VMEM)] * count,
        out_shape=[jax.ShapeDtypeStruct(weight.shape, weight.dtype) for weight in weights],
        scratch_shapes=[pltpu.SemaphoreType.DMA((count,))],
        cost_estimate=pl.CostEstimate(
            flops=0,
            bytes_accessed=sum(2 * weight.size * weight.dtype.itemsize for weight in weights),
            transcendentals=0,
        ),
        compiler_params=pltpu.CompilerParams(vmem_limit_bytes=16 << 20),
    )(*[pltpu.with_memory_space_constraint(weight, pltpu.HBM) for weight in weights])


def rows_times(rows, mats):
    quarter = mats[0].shape[0]
    total = None
    for j, mat in enumerate(mats):
        part = jnp.dot(
            rows[:, j * quarter : (j + 1) * quarter], mat, preferred_element_type=jnp.float32
        )
        total = part if total is None else total + part
    return total


def contract_cols(left, right):
    return lax.dot_general(
        left, right, (((1,), (1,)), ((), ())), preferred_element_type=jnp.float32
    )


def on_device(
    fwd_tokens,
    fwd_routes,
    fwd_gates,
    bwd_tokens,
    bwd_grads,
    bwd_routes,
    bwd_gates,
    gate_proj,
    up_proj,
    down_proj,
):
    experts = lax.axis_size("ep") // QUARTERS
    tokens = fwd_tokens.shape[1]
    slot_cap = 3 * tokens // (2 * experts)
    me = lax.axis_index("ep")
    section = lax.axis_index("pp")
    place = me // QUARTERS
    inner = is_inner(place) if experts == 4 else jnp.zeros_like(place)
    where = jnp.stack([place, me % QUARTERS, section, inner]).astype(jnp.int32)

    gate, up, down = gate_proj[0, 0], up_proj[0, 0], down_proj[0, 0]
    gate_across = paired(gate, 2)
    up_across = paired(up, 2)
    gate_beside = paired(gate, 1)
    up_beside = paired(up, 1)
    down_beside = paired(down, 1)
    fwd_spread, row_spread, grad_spread = spread(
        after(where, gate_beside),
        fwd_routes[0],
        bwd_routes[0],
        bwd_gates[0],
        (fwd_tokens[0], bwd_tokens[0], bwd_grads[0]),
        slot_cap,
        experts,
    )
    order = sorted(range(1, experts), reverse=True)
    distances = sent_distances(experts)
    last = order[-1]
    fwd_blocks, bwd_blocks, grad_blocks = {}, {}, {}
    for d in order:
        before = (up_beside, down_beside) if d == last else ()
        fwd_blocks[d] = sent(fwd_spread[d], distances[d], *before)
    for d in order:
        bwd_blocks[d] = sent(row_spread[d], distances[d], fwd_blocks[d])
    down_across = paired(down, 2, gate_across)
    gate_diagonal = paired(gate_across, 1, bwd_blocks[last])
    up_diagonal = paired(up_across, 1, bwd_blocks[last])
    for d in order:
        before = (gate_diagonal, up_diagonal) if d == last else (up_across,)
        grad_blocks[d] = sent(grad_spread[d], distances[d], bwd_blocks[d], *before)
    down_diagonal = paired(down_across, 1, up_diagonal)
    near = lax.optimization_barrier((gate_across, down_beside, fwd_blocks[last]))
    gate_across, down_beside = staged(near[:2])
    near = lax.optimization_barrier((up_across, bwd_blocks[last]))
    (up_across,) = staged(near[:1])
    gate_mats = [gate, gate_beside, gate_across, gate_diagonal]
    up_mats = [up, up_beside, up_across, up_diagonal]
    down_mats = [down, down_beside, down_across, down_diagonal]
    fwd_blocks = [fwd_spread[0]] + [fwd_blocks[d] for d in range(1, experts)]
    bwd_blocks = [row_spread[0]] + [bwd_blocks[d] for d in range(1, experts)]
    grad_blocks = [grad_spread[0]] + [grad_blocks[d] for d in range(1, experts)]

    rows = jnp.concatenate(fwd_blocks)
    gate_value, up_value = rows_times(rows, gate_mats), rows_times(rows, up_mats)
    hidden = (jax.nn.silu(gate_value) * up_value).astype(jnp.bfloat16)
    fwd_parts = [
        jnp.dot(hidden, mat, preferred_element_type=jnp.float32).astype(jnp.bfloat16)
        for mat in down_mats
    ]

    rows = jnp.concatenate(bwd_blocks)
    gate_value, up_value = rows_times(rows, gate_mats), rows_times(rows, up_mats)
    sigmoid_value = jax.nn.sigmoid(gate_value)
    gate_factor = up_value * sigmoid_value * (1.0 + gate_value * (1.0 - sigmoid_value))
    up_factor = gate_value * sigmoid_value

    landed = lax.optimization_barrier((*grad_blocks[1:], gate_factor, up_factor, *fwd_parts))
    grads = jnp.concatenate([grad_blocks[0], *landed[: experts - 1]])
    quarter = down.shape[1]
    grad_hidden = sum(
        contract_cols(grads[:, j * quarter : (j + 1) * quarter], mat)
        for j, mat in enumerate(down_mats)
    )
    grad_gate = (grad_hidden * landed[experts - 1]).astype(jnp.bfloat16)
    grad_up = (grad_hidden * landed[experts]).astype(jnp.bfloat16)
    bwd_parts = [
        (contract_cols(grad_gate, g) + contract_cols(grad_up, u)).astype(jnp.bfloat16)
        for g, u in zip(gate_mats, up_mats)
    ]
    fwd_parts = landed[experts + 1 :]
    merged = lax.axis_size("pp") == 2

    done = tuple(grad_blocks[1:])
    fwd_meta = jnp.concatenate(
        [fwd_routes[0].reshape(1, tokens).astype(jnp.float32), fwd_gates[0].reshape(1, tokens)]
    )
    bwd_meta = bwd_routes[0].reshape(1, tokens).astype(jnp.float32)
    bwd_meta = jnp.concatenate([bwd_meta, jnp.ones_like(bwd_meta)])

    def returned(parts, steps):
        out = jnp.concatenate(parts, axis=1)
        blocks = [out[d * slot_cap : (d + 1) * slot_cap] for d in range(experts)]
        if experts == 4:
            edge = jnp.where(inner == 1, blocks[0], blocks[3])
            core = jnp.where(inner == 1, blocks[3], blocks[0])
            blocks = [edge, blocks[2], blocks[1], core]
        return [handed(b, steps, d) for b, d in zip(blocks, handed_distances(experts))]

    if merged:
        first = section == 0
        meta = handed(after(jnp.where(first, fwd_meta, bwd_meta), *done), (1, -1), (0, 0))
        parts = [jnp.where(first, fwd, bwd) for fwd, bwd in zip(fwd_parts, bwd_parts)]
        handed_forward, handed_backward = collect(where, meta, returned(parts, (1, -1)), 2)
    else:
        metas = [handed(after(m, *done), (by,), (0, 0)) for m, by in ((fwd_meta, 1), (bwd_meta, -1))]
        (handed_forward,) = collect(where, metas[0], returned(fwd_parts, (1,)), 1)
        (handed_backward,) = collect(where, metas[1], returned(bwd_parts, (-1,)), 1)
    return handed_forward[None], handed_backward[None]


def solution(mesh):
    return jax.shard_map(
        on_device,
        mesh=mesh,
        in_specs=(P("pp", "ep", None),) * 7 + (P("pp", "ep", None, None),) * 3,
        out_specs=(P("pp", "ep", None), P("pp", "ep", None)),
        check_vma=False,
    )
```

```python
import functools

import jax
import jax.numpy as jnp
from jax import lax
from jax.experimental import pallas as pl
from jax.experimental.pallas import tpu as pltpu
from jax.sharding import PartitionSpec as P

QUARTERS = 4


def is_inner(place):
    return (place ^ (place >> 1)) & 1


def sent_distances(experts):
    if experts == 4:
        return ((0, 0), (2, 1), (1, 2), (3, 3))
    return tuple((d, d) for d in range(experts))


def handed_distances(experts):
    if experts == 4:
        return ((3, 0), (2, 1), (1, 2), (0, 3))
    return tuple((d, d) for d in range(experts))


def landed_distances(experts):
    if experts == 4:
        return ((3, 0), (1, 2), (2, 1), (0, 3))
    return tuple((d, d) for d in range(experts))


def expert_at(where_ref, distance):
    outer, inner = distance
    return where_ref[0] ^ (outer + where_ref[3] * (inner - outer))


def target(index, distance):
    return index ^ (QUARTERS * distance[is_inner(index // QUARTERS)])


def after(block, *done):
    return lax.optimization_barrier((block, *done))[0] if done else block


def paired(block, distance, *done):
    block = after(block, *done)
    count = lax.axis_size("ep")
    return lax.ppermute(block, "ep", [(i, i ^ distance) for i in range(count)])


def sent(block, distance, *done):
    block = after(block, *done)
    count = lax.axis_size("ep")
    return lax.ppermute(block, "ep", [(i, target(i, distance)) for i in range(count)])


def handed(block, steps, distance):
    sections, count = lax.axis_size("pp"), lax.axis_size("ep")
    route = [
        (s * count + i, (s + by) * count + target(i, distance))
        for s in range(sections)
        for by in steps
        if 0 <= s + by < sections
        for i in range(count)
    ]
    return lax.ppermute(block, ("pp", "ep"), route)


def slot_matrix(route, expert_of, slot_cap, experts):
    count = route.shape[1]
    named = [route == expert_of(distance) for distance in range(experts)]
    hits = [jnp.where(one, 1.0, 0.0) for one in named]
    hits += [jnp.zeros_like(hits[0])] * (-experts % 8)
    low = lax.broadcasted_iota(jnp.int32, (count, count), 0)
    high = lax.broadcasted_iota(jnp.int32, (count, count), 1)
    earlier = jnp.where(low < high, 1.0, 0.0).astype(jnp.bfloat16)
    place = jnp.dot(
        jnp.concatenate(hits).astype(jnp.bfloat16), earlier, preferred_element_type=jnp.float32
    ).astype(jnp.int32)
    slots = lax.broadcasted_iota(jnp.int32, (slot_cap, count), 0)
    return jnp.concatenate(
        [jnp.where((slots == place[d : d + 1]) & named[d], 1.0, 0.0) for d in range(experts)]
    )


def spread_kernel(slot_cap, experts, where_ref, fwd_ref, bwd_ref, gate_ref, *refs):
    value_refs, out_refs = refs[:3], refs[3:]
    quarter = value_refs[0].shape[1] // QUARTERS
    fwd_slots, bwd_slots = [
        slot_matrix(ref[...], lambda d: expert_at(where_ref, sent_distances(experts)[d]), slot_cap, experts)
        for ref in (fwd_ref, bwd_ref)
    ]
    slot_gate = jnp.sum(bwd_slots * gate_ref[...], axis=1, keepdims=True)
    fwd_slots, bwd_slots = fwd_slots.astype(jnp.bfloat16), bwd_slots.astype(jnp.bfloat16)
    for at, chosen in enumerate((fwd_slots, bwd_slots, bwd_slots)):
        for j in range(QUARTERS):
            start = pl.multiple_of((where_ref[1] ^ j) * quarter, quarter)
            values = value_refs[at][:, pl.ds(start, quarter)]
            rows = jnp.dot(chosen, values, preferred_element_type=jnp.float32)
            if at == 2:
                rows = rows * slot_gate
            for d in range(experts):
                out_refs[at * experts + d][:, j * quarter : (j + 1) * quarter] = rows[
                    d * slot_cap : (d + 1) * slot_cap
                ].astype(jnp.bfloat16)


def spread(where, fwd_routes, bwd_routes, gates, values, slot_cap, experts):
    tokens, width = values[0].shape
    args = [*(row.reshape(1, tokens) for row in (fwd_routes, bwd_routes, gates)), *values]
    out_count = experts * len(values)
    vmem = pl.BlockSpec(memory_space=pltpu.VMEM)
    out = pl.pallas_call(
        functools.partial(spread_kernel, slot_cap, experts),
        in_specs=[pl.BlockSpec(memory_space=pltpu.SMEM)] + [vmem] * len(args),
        out_specs=[vmem] * out_count,
        out_shape=[jax.ShapeDtypeStruct((slot_cap, width), jnp.bfloat16)] * out_count,
        cost_estimate=pl.CostEstimate(
            flops=2 * out_count * slot_cap * tokens * width,
            bytes_accessed=2 * width * (tokens * len(values) + out_count * slot_cap),
            transcendentals=0,
        ),
        compiler_params=pltpu.CompilerParams(vmem_limit_bytes=20 << 20),
    )(where, *[pltpu.with_memory_space_constraint(arg, pltpu.HBM) for arg in args])
    return [out[at * experts : (at + 1) * experts] for at in range(len(values))]


def collect_kernel(slot_cap, experts, where_ref, meta_ref, *refs):
    block_refs, out_refs, (held, stored) = refs[:experts], refs[experts:-2], refs[-2:]
    tokens = meta_ref.shape[1]
    quarter = out_refs[0].shape[1] // QUARTERS
    low = lax.broadcasted_iota(jnp.int32, (tokens, tokens), 1)
    high = lax.broadcasted_iota(jnp.int32, (tokens, tokens), 0)
    route, gate = [
        jnp.sum(jnp.where(low == high, meta_ref[at : at + 1], 0.0), axis=1, keepdims=True)
        for at in range(2)
    ]
    lane = lax.broadcasted_iota(jnp.int32, (1, 128), 1)
    relative = jnp.full((1, 128), -1, jnp.int32)
    for d, distance in enumerate(landed_distances(experts)):
        relative = jnp.where(lane == d, expert_at(where_ref, distance), relative)
    hits = jnp.where(route == relative.astype(jnp.float32), 1.0, 0.0)
    earlier = jnp.where(low < high, 1.0, 0.0).astype(jnp.bfloat16)
    place = jnp.dot(earlier, hits.astype(jnp.bfloat16), preferred_element_type=jnp.float32)
    slots = lax.broadcasted_iota(jnp.int32, (tokens, slot_cap), 1).astype(jnp.float32)
    chosen = jnp.concatenate(
        [
            jnp.where((slots == place[:, d : d + 1]) & (hits[:, d : d + 1] > 0.0), 1.0, 0.0)
            for d in range(experts)
        ],
        axis=1,
    ).astype(jnp.bfloat16)
    copies = []
    for j in range(QUARTERS):
        part = slice(j * quarter, (j + 1) * quarter)
        rows = jnp.concatenate([ref[:, part] for ref in block_refs])
        total = jnp.dot(chosen, rows, preferred_element_type=jnp.float32) * gate
        if len(out_refs) == 1:
            results = [total]
        else:
            first = where_ref[2] == 0
            results = [jnp.where(first, 0.0, total), jnp.where(first, total, 0.0)]
        start = pl.multiple_of((where_ref[1] ^ j) * quarter, quarter)
        for at, result in enumerate(results):
            held[at, j] = result.astype(jnp.bfloat16)
            goal = out_refs[at].at[:, pl.ds(start, quarter)]
            copies.append(pltpu.make_async_copy(held.at[at, j], goal, stored.at[at, j]))
            copies[-1].start()
    for copy in copies:
        copy.wait()


def collect(where, meta, blocks, outputs):
    tokens = meta.shape[1]
    experts = len(blocks)
    slot_cap, width = blocks[0].shape
    quarter = width // QUARTERS
    vmem = pl.BlockSpec(memory_space=pltpu.VMEM)
    return pl.pallas_call(
        functools.partial(collect_kernel, slot_cap, experts),
        in_specs=[pl.BlockSpec(memory_space=pltpu.SMEM)] + [vmem] * (1 + experts),
        out_specs=[pl.BlockSpec(memory_space=pl.ANY)] * outputs,
        scratch_shapes=[
            pltpu.VMEM((outputs, QUARTERS, tokens, quarter), jnp.bfloat16),
            pltpu.SemaphoreType.DMA((outputs, QUARTERS)),
        ],
        out_shape=[jax.ShapeDtypeStruct((tokens, width), jnp.bfloat16)] * outputs,
        cost_estimate=pl.CostEstimate(
            flops=2 * experts * slot_cap * tokens * width,
            bytes_accessed=2 * width * (tokens * outputs + experts * slot_cap),
            transcendentals=0,
        ),
        compiler_params=pltpu.CompilerParams(vmem_limit_bytes=16 << 20),
    )(where, meta, *blocks)


def stage_kernel(*refs):
    count = len(refs) // 2
    arrived = refs[-1]
    copies = [
        pltpu.make_async_copy(refs[at], refs[count + at], arrived.at[at]) for at in range(count)
    ]
    for copy in copies:
        copy.start()
    for copy in copies:
        copy.wait()


def staged(weights):
    count = len(weights)
    return pl.pallas_call(
        stage_kernel,
        in_specs=[pl.BlockSpec(memory_space=pl.ANY)] * count,
        out_specs=[pl.BlockSpec(memory_space=pltpu.VMEM)] * count,
        out_shape=[jax.ShapeDtypeStruct(weight.shape, weight.dtype) for weight in weights],
        scratch_shapes=[pltpu.SemaphoreType.DMA((count,))],
        cost_estimate=pl.CostEstimate(
            flops=0,
            bytes_accessed=sum(2 * weight.size * weight.dtype.itemsize for weight in weights),
            transcendentals=0,
        ),
        compiler_params=pltpu.CompilerParams(vmem_limit_bytes=16 << 20),
    )(*[pltpu.with_memory_space_constraint(weight, pltpu.HBM) for weight in weights])


def turn_kernel(*refs):
    count = len(refs) // 2
    for at in range(count):
        refs[count + at][...] = refs[at][...].T


def turned(mats):
    vmem = pl.BlockSpec(memory_space=pltpu.VMEM)
    return pl.pallas_call(
        turn_kernel,
        in_specs=[vmem] * len(mats),
        out_specs=[vmem] * len(mats),
        out_shape=[jax.ShapeDtypeStruct(mat.shape[::-1], mat.dtype) for mat in mats],
        cost_estimate=pl.CostEstimate(
            flops=0,
            bytes_accessed=sum(2 * mat.size * mat.dtype.itemsize for mat in mats),
            transcendentals=0,
        ),
        compiler_params=pltpu.CompilerParams(vmem_limit_bytes=16 << 20),
    )(*mats)


def rows_times(rows, mats):
    quarter = mats[0].shape[0]
    total = None
    for j, mat in enumerate(mats):
        part = jnp.dot(
            rows[:, j * quarter : (j + 1) * quarter], mat, preferred_element_type=jnp.float32
        )
        total = part if total is None else total + part
    return total


def contract_cols(left, right):
    return lax.dot_general(
        left, right, (((1,), (1,)), ((), ())), preferred_element_type=jnp.float32
    )


def on_device(
    fwd_tokens,
    fwd_routes,
    fwd_gates,
    bwd_tokens,
    bwd_grads,
    bwd_routes,
    bwd_gates,
    gate_proj,
    up_proj,
    down_proj,
):
    experts = lax.axis_size("ep") // QUARTERS
    tokens = fwd_tokens.shape[1]
    slot_cap = 3 * tokens // (2 * experts)
    me = lax.axis_index("ep")
    section = lax.axis_index("pp")
    place = me // QUARTERS
    inner = is_inner(place) if experts == 4 else jnp.zeros_like(place)
    where = jnp.stack([place, me % QUARTERS, section, inner]).astype(jnp.int32)

    gate, up, down = gate_proj[0, 0], up_proj[0, 0], down_proj[0, 0]
    gate_across = paired(gate, 2)
    up_across = paired(up, 2)
    gate_beside = paired(gate, 1)
    up_beside = paired(up, 1)
    down_beside = paired(down, 1)
    fwd_spread, row_spread, grad_spread = spread(
        after(where, gate_beside),
        fwd_routes[0],
        bwd_routes[0],
        bwd_gates[0],
        (fwd_tokens[0], bwd_tokens[0], bwd_grads[0]),
        slot_cap,
        experts,
    )
    order = sorted(range(1, experts), reverse=True)
    distances = sent_distances(experts)
    last = order[-1]
    fwd_blocks, bwd_blocks, grad_blocks = {}, {}, {}
    for d in order:
        before = (up_beside, down_beside) if d == last else ()
        fwd_blocks[d] = sent(fwd_spread[d], distances[d], *before)
    for d in order:
        bwd_blocks[d] = sent(row_spread[d], distances[d], fwd_blocks[d])
    down_across = paired(down, 2, gate_across)
    gate_diagonal = paired(gate_across, 1, bwd_blocks[last])
    up_diagonal = paired(up_across, 1, bwd_blocks[last])
    for d in order:
        before = ()
        grad_blocks[d] = sent(grad_spread[d], distances[d], bwd_blocks[d], *before)
    near = lax.optimization_barrier((gate_across, down_beside, fwd_blocks[last]))
    gate_across, down_beside = staged(near[:2])
    near = lax.optimization_barrier((up_across, bwd_blocks[last]))
    (up_across,) = staged(near[:1])
    gate_mats = [gate, gate_beside, gate_across, gate_diagonal]
    up_mats = [up, up_beside, up_across, up_diagonal]
    fwd_blocks = [fwd_spread[0]] + [fwd_blocks[d] for d in range(1, experts)]
    bwd_blocks = [row_spread[0]] + [bwd_blocks[d] for d in range(1, experts)]
    grad_blocks = [grad_spread[0]] + [grad_blocks[d] for d in range(1, experts)]

    rows = jnp.concatenate(fwd_blocks)
    gate_value, up_value = rows_times(rows, gate_mats), rows_times(rows, up_mats)
    hidden = (jax.nn.silu(gate_value) * up_value).astype(jnp.bfloat16)
    ready = lax.optimization_barrier((*gate_mats, *up_mats, hidden))[: 2 * QUARTERS]
    turned_mats = turned(ready)
    down_across = after(down_across, turned_mats[0])
    down_diagonal = paired(down_across, 1)
    down_mats = [down, down_beside, down_across, down_diagonal]
    fwd_parts = [
        jnp.dot(hidden, mat, preferred_element_type=jnp.float32).astype(jnp.bfloat16)
        for mat in down_mats
    ]

    rows = jnp.concatenate(bwd_blocks)
    gate_value, up_value = rows_times(rows, gate_mats), rows_times(rows, up_mats)
    sigmoid_value = jax.nn.sigmoid(gate_value)
    gate_factor = up_value * sigmoid_value * (1.0 + gate_value * (1.0 - sigmoid_value))
    up_factor = gate_value * sigmoid_value

    landed = lax.optimization_barrier((*grad_blocks[1:], gate_factor, up_factor, *fwd_parts))
    grads = jnp.concatenate([grad_blocks[0], *landed[: experts - 1]])
    quarter = down.shape[1]
    grad_hidden = sum(
        contract_cols(grads[:, j * quarter : (j + 1) * quarter], mat)
        for j, mat in enumerate(down_mats)
    )
    grad_gate = (grad_hidden * landed[experts - 1]).astype(jnp.bfloat16)
    grad_up = (grad_hidden * landed[experts]).astype(jnp.bfloat16)
    bwd_parts = [
        (
            jnp.dot(grad_gate, g, preferred_element_type=jnp.float32)
            + jnp.dot(grad_up, u, preferred_element_type=jnp.float32)
        ).astype(jnp.bfloat16)
        for g, u in zip(turned_mats[:QUARTERS], turned_mats[QUARTERS:])
    ]
    fwd_parts = landed[experts + 1 :]
    merged = lax.axis_size("pp") == 2

    done = tuple(grad_blocks[1:])
    fwd_meta = jnp.concatenate(
        [fwd_routes[0].reshape(1, tokens).astype(jnp.float32), fwd_gates[0].reshape(1, tokens)]
    )
    bwd_meta = bwd_routes[0].reshape(1, tokens).astype(jnp.float32)
    bwd_meta = jnp.concatenate([bwd_meta, jnp.ones_like(bwd_meta)])

    def returned(parts, steps):
        out = jnp.concatenate(parts, axis=1)
        blocks = [out[d * slot_cap : (d + 1) * slot_cap] for d in range(experts)]
        if experts == 4:
            edge = jnp.where(inner == 1, blocks[0], blocks[3])
            core = jnp.where(inner == 1, blocks[3], blocks[0])
            blocks = [edge, blocks[2], blocks[1], core]
        return [handed(b, steps, d) for b, d in zip(blocks, handed_distances(experts))]

    if merged:
        first = section == 0
        meta = handed(after(jnp.where(first, fwd_meta, bwd_meta), *done), (1, -1), (0, 0))
        parts = [jnp.where(first, fwd, bwd) for fwd, bwd in zip(fwd_parts, bwd_parts)]
        handed_forward, handed_backward = collect(where, meta, returned(parts, (1, -1)), 2)
    else:
        metas = [handed(after(m, *done), (by,), (0, 0)) for m, by in ((fwd_meta, 1), (bwd_meta, -1))]
        (handed_forward,) = collect(where, metas[0], returned(fwd_parts, (1,)), 1)
        (handed_backward,) = collect(where, metas[1], returned(bwd_parts, (-1,)), 1)
    return handed_forward[None], handed_backward[None]


def solution(mesh):
    return jax.shard_map(
        on_device,
        mesh=mesh,
        in_specs=(P("pp", "ep", None),) * 7 + (P("pp", "ep", None, None),) * 3,
        out_specs=(P("pp", "ep", None), P("pp", "ep", None)),
        check_vma=False,
    )
```

```python
import functools

import jax
import jax.numpy as jnp
from jax import lax
from jax.experimental import pallas as pl
from jax.experimental.pallas import tpu as pltpu
from jax.sharding import PartitionSpec as P

QUARTERS = 4


def is_inner(place):
    return (place ^ (place >> 1)) & 1


def sent_distances(experts):
    if experts == 4:
        return ((0, 0), (2, 1), (1, 2), (3, 3))
    return tuple((d, d) for d in range(experts))


def handed_distances(experts):
    if experts == 4:
        return ((3, 0), (2, 1), (1, 2), (0, 3))
    return tuple((d, d) for d in range(experts))


def landed_distances(experts):
    if experts == 4:
        return ((3, 0), (1, 2), (2, 1), (0, 3))
    return tuple((d, d) for d in range(experts))


def expert_at(where_ref, distance):
    outer, inner = distance
    return where_ref[0] ^ (outer + where_ref[3] * (inner - outer))


def target(index, distance):
    return index ^ (QUARTERS * distance[is_inner(index // QUARTERS)])


def after(block, *done):
    return lax.optimization_barrier((block, *done))[0] if done else block


def paired(block, distance, *done):
    block = after(block, *done)
    count = lax.axis_size("ep")
    return lax.ppermute(block, "ep", [(i, i ^ distance) for i in range(count)])


def sent(block, distance, *done):
    block = after(block, *done)
    count = lax.axis_size("ep")
    return lax.ppermute(block, "ep", [(i, target(i, distance)) for i in range(count)])


def handed(block, steps, distance):
    sections, count = lax.axis_size("pp"), lax.axis_size("ep")
    route = [
        (s * count + i, (s + by) * count + target(i, distance))
        for s in range(sections)
        for by in steps
        if 0 <= s + by < sections
        for i in range(count)
    ]
    return lax.ppermute(block, ("pp", "ep"), route)


def slot_matrix(route, expert_of, slot_cap, experts):
    count = route.shape[1]
    named = [route == expert_of(distance) for distance in range(experts)]
    hits = [jnp.where(one, 1.0, 0.0) for one in named]
    hits += [jnp.zeros_like(hits[0])] * (-experts % 8)
    low = lax.broadcasted_iota(jnp.int32, (count, count), 0)
    high = lax.broadcasted_iota(jnp.int32, (count, count), 1)
    earlier = jnp.where(low < high, 1.0, 0.0).astype(jnp.bfloat16)
    place = jnp.dot(
        jnp.concatenate(hits).astype(jnp.bfloat16), earlier, preferred_element_type=jnp.float32
    ).astype(jnp.int32)
    slots = lax.broadcasted_iota(jnp.int32, (slot_cap, count), 0)
    return jnp.concatenate(
        [jnp.where((slots == place[d : d + 1]) & named[d], 1.0, 0.0) for d in range(experts)]
    )


def spread_kernel(slot_cap, experts, where_ref, fwd_ref, bwd_ref, gate_ref, *refs):
    value_refs, out_refs = refs[:3], refs[3:]
    quarter = value_refs[0].shape[1] // QUARTERS
    fwd_slots, bwd_slots = [
        slot_matrix(ref[...], lambda d: expert_at(where_ref, sent_distances(experts)[d]), slot_cap, experts)
        for ref in (fwd_ref, bwd_ref)
    ]
    slot_gate = jnp.sum(bwd_slots * gate_ref[...], axis=1, keepdims=True)
    fwd_slots, bwd_slots = fwd_slots.astype(jnp.bfloat16), bwd_slots.astype(jnp.bfloat16)
    for at, chosen in enumerate((fwd_slots, bwd_slots, bwd_slots)):
        for j in range(QUARTERS):
            start = pl.multiple_of((where_ref[1] ^ j) * quarter, quarter)
            values = value_refs[at][:, pl.ds(start, quarter)]
            rows = jnp.dot(chosen, values, preferred_element_type=jnp.float32)
            if at == 2:
                rows = rows * slot_gate
            for d in range(experts):
                out_refs[at * experts + d][:, j * quarter : (j + 1) * quarter] = rows[
                    d * slot_cap : (d + 1) * slot_cap
                ].astype(jnp.bfloat16)


def spread(where, fwd_routes, bwd_routes, gates, values, slot_cap, experts):
    tokens, width = values[0].shape
    args = [*(row.reshape(1, tokens) for row in (fwd_routes, bwd_routes, gates)), *values]
    out_count = experts * len(values)
    vmem = pl.BlockSpec(memory_space=pltpu.VMEM)
    out = pl.pallas_call(
        functools.partial(spread_kernel, slot_cap, experts),
        in_specs=[pl.BlockSpec(memory_space=pltpu.SMEM)] + [vmem] * len(args),
        out_specs=[vmem] * out_count,
        out_shape=[jax.ShapeDtypeStruct((slot_cap, width), jnp.bfloat16)] * out_count,
        cost_estimate=pl.CostEstimate(
            flops=2 * out_count * slot_cap * tokens * width,
            bytes_accessed=2 * width * (tokens * len(values) + out_count * slot_cap),
            transcendentals=0,
        ),
        compiler_params=pltpu.CompilerParams(vmem_limit_bytes=20 << 20),
    )(where, *[pltpu.with_memory_space_constraint(arg, pltpu.HBM) for arg in args])
    return [out[at * experts : (at + 1) * experts] for at in range(len(values))]


def collect_kernel(slot_cap, experts, where_ref, meta_ref, *refs):
    block_refs, out_refs, (held, stored) = refs[:experts], refs[experts:-2], refs[-2:]
    tokens = meta_ref.shape[1]
    quarter = out_refs[0].shape[1] // QUARTERS
    low = lax.broadcasted_iota(jnp.int32, (tokens, tokens), 1)
    high = lax.broadcasted_iota(jnp.int32, (tokens, tokens), 0)
    route, gate = [
        jnp.sum(jnp.where(low == high, meta_ref[at : at + 1], 0.0), axis=1, keepdims=True)
        for at in range(2)
    ]
    lane = lax.broadcasted_iota(jnp.int32, (1, 128), 1)
    relative = jnp.full((1, 128), -1, jnp.int32)
    for d, distance in enumerate(landed_distances(experts)):
        relative = jnp.where(lane == d, expert_at(where_ref, distance), relative)
    hits = jnp.where(route == relative.astype(jnp.float32), 1.0, 0.0)
    earlier = jnp.where(low < high, 1.0, 0.0).astype(jnp.bfloat16)
    place = jnp.dot(earlier, hits.astype(jnp.bfloat16), preferred_element_type=jnp.float32)
    slots = lax.broadcasted_iota(jnp.int32, (tokens, slot_cap), 1).astype(jnp.float32)
    chosen = jnp.concatenate(
        [
            jnp.where((slots == place[:, d : d + 1]) & (hits[:, d : d + 1] > 0.0), 1.0, 0.0)
            for d in range(experts)
        ],
        axis=1,
    ).astype(jnp.bfloat16)
    copies = []
    for j in range(QUARTERS):
        part = slice(j * quarter, (j + 1) * quarter)
        rows = jnp.concatenate([ref[:, part] for ref in block_refs])
        total = jnp.dot(chosen, rows, preferred_element_type=jnp.float32) * gate
        if len(out_refs) == 1:
            results = [total]
        else:
            first = where_ref[2] == 0
            results = [jnp.where(first, 0.0, total), jnp.where(first, total, 0.0)]
        start = pl.multiple_of((where_ref[1] ^ j) * quarter, quarter)
        for at, result in enumerate(results):
            held[at, j] = result.astype(jnp.bfloat16)
            goal = out_refs[at].at[:, pl.ds(start, quarter)]
            copies.append(pltpu.make_async_copy(held.at[at, j], goal, stored.at[at, j]))
            copies[-1].start()
    for copy in copies:
        copy.wait()


def collect(where, meta, blocks, outputs):
    tokens = meta.shape[1]
    experts = len(blocks)
    slot_cap, width = blocks[0].shape
    quarter = width // QUARTERS
    vmem = pl.BlockSpec(memory_space=pltpu.VMEM)
    return pl.pallas_call(
        functools.partial(collect_kernel, slot_cap, experts),
        in_specs=[pl.BlockSpec(memory_space=pltpu.SMEM)] + [vmem] * (1 + experts),
        out_specs=[pl.BlockSpec(memory_space=pl.ANY)] * outputs,
        scratch_shapes=[
            pltpu.VMEM((outputs, QUARTERS, tokens, quarter), jnp.bfloat16),
            pltpu.SemaphoreType.DMA((outputs, QUARTERS)),
        ],
        out_shape=[jax.ShapeDtypeStruct((tokens, width), jnp.bfloat16)] * outputs,
        cost_estimate=pl.CostEstimate(
            flops=2 * experts * slot_cap * tokens * width,
            bytes_accessed=2 * width * (tokens * outputs + experts * slot_cap),
            transcendentals=0,
        ),
        compiler_params=pltpu.CompilerParams(vmem_limit_bytes=16 << 20),
    )(where, meta, *blocks)


def stage_kernel(*refs):
    count = len(refs) // 2
    arrived = refs[-1]
    copies = [
        pltpu.make_async_copy(refs[at], refs[count + at], arrived.at[at]) for at in range(count)
    ]
    for copy in copies:
        copy.start()
    for copy in copies:
        copy.wait()


def staged(weights):
    count = len(weights)
    return pl.pallas_call(
        stage_kernel,
        in_specs=[pl.BlockSpec(memory_space=pl.ANY)] * count,
        out_specs=[pl.BlockSpec(memory_space=pltpu.VMEM)] * count,
        out_shape=[jax.ShapeDtypeStruct(weight.shape, weight.dtype) for weight in weights],
        scratch_shapes=[pltpu.SemaphoreType.DMA((count,))],
        cost_estimate=pl.CostEstimate(
            flops=0,
            bytes_accessed=sum(2 * weight.size * weight.dtype.itemsize for weight in weights),
            transcendentals=0,
        ),
        compiler_params=pltpu.CompilerParams(vmem_limit_bytes=16 << 20),
    )(*[pltpu.with_memory_space_constraint(weight, pltpu.HBM) for weight in weights])


def turn_kernel(*refs):
    count = len(refs) // 2
    for at in range(count):
        refs[count + at][...] = refs[at][...].T


def turned(mats):
    vmem = pl.BlockSpec(memory_space=pltpu.VMEM)
    return pl.pallas_call(
        turn_kernel,
        in_specs=[vmem] * len(mats),
        out_specs=[vmem] * len(mats),
        out_shape=[jax.ShapeDtypeStruct(mat.shape[::-1], mat.dtype) for mat in mats],
        cost_estimate=pl.CostEstimate(
            flops=0,
            bytes_accessed=sum(2 * mat.size * mat.dtype.itemsize for mat in mats),
            transcendentals=0,
        ),
        compiler_params=pltpu.CompilerParams(vmem_limit_bytes=16 << 20),
    )(*mats)


def rows_times(rows, mats):
    quarter = mats[0].shape[0]
    total = None
    for j, mat in enumerate(mats):
        part = jnp.dot(
            rows[:, j * quarter : (j + 1) * quarter], mat, preferred_element_type=jnp.float32
        )
        total = part if total is None else total + part
    return total


def contract_cols(left, right):
    return lax.dot_general(
        left, right, (((1,), (1,)), ((), ())), preferred_element_type=jnp.float32
    )


def on_device(
    fwd_tokens,
    fwd_routes,
    fwd_gates,
    bwd_tokens,
    bwd_grads,
    bwd_routes,
    bwd_gates,
    gate_proj,
    up_proj,
    down_proj,
):
    experts = lax.axis_size("ep") // QUARTERS
    tokens = fwd_tokens.shape[1]
    slot_cap = 3 * tokens // (2 * experts)
    me = lax.axis_index("ep")
    section = lax.axis_index("pp")
    place = me // QUARTERS
    inner = is_inner(place) if experts == 4 else jnp.zeros_like(place)
    where = jnp.stack([place, me % QUARTERS, section, inner]).astype(jnp.int32)

    gate, up, down = gate_proj[0, 0], up_proj[0, 0], down_proj[0, 0]
    gate_across = paired(gate, 2)
    up_across = paired(up, 2)
    gate_beside = paired(gate, 1)
    up_beside = paired(up, 1)
    down_beside = paired(down, 1)
    fwd_spread, row_spread, grad_spread = spread(
        after(where, gate_beside),
        fwd_routes[0],
        bwd_routes[0],
        bwd_gates[0],
        (fwd_tokens[0], bwd_tokens[0], bwd_grads[0]),
        slot_cap,
        experts,
    )
    order = sorted(range(1, experts), reverse=True)
    distances = sent_distances(experts)
    last = order[-1]
    fwd_blocks, bwd_blocks, grad_blocks = {}, {}, {}
    for d in order:
        before = (up_beside, down_beside) if d == last else ()
        fwd_blocks[d] = sent(fwd_spread[d], distances[d], *before)
    for d in order:
        bwd_blocks[d] = sent(row_spread[d], distances[d], fwd_blocks[d])
    down_across = paired(down, 2, gate_across)
    gate_diagonal = paired(gate_across, 1, bwd_blocks[last])
    up_diagonal = paired(up_across, 1, bwd_blocks[last])
    for d in order:
        before = ()
        grad_blocks[d] = sent(grad_spread[d], distances[d], bwd_blocks[d], *before)
    near = lax.optimization_barrier((gate_across, down_beside, fwd_blocks[last]))
    gate_across, down_beside = staged(near[:2])
    near = lax.optimization_barrier((up_across, bwd_blocks[last]))
    (up_across,) = staged(near[:1])
    gate_mats = [gate, gate_beside, gate_across, gate_diagonal]
    up_mats = [up, up_beside, up_across, up_diagonal]
    fwd_blocks = [fwd_spread[0]] + [fwd_blocks[d] for d in range(1, experts)]
    bwd_blocks = [row_spread[0]] + [bwd_blocks[d] for d in range(1, experts)]
    grad_blocks = [grad_spread[0]] + [grad_blocks[d] for d in range(1, experts)]

    rows = jnp.concatenate(fwd_blocks)
    gate_value, up_value = rows_times(rows, gate_mats), rows_times(rows, up_mats)
    hidden = (jax.nn.silu(gate_value) * up_value).astype(jnp.bfloat16)
    ready = lax.optimization_barrier((*gate_mats, *up_mats, down, down_beside, hidden))[:-1]
    *turned_mats, down_turned, beside_turned = turned(ready)
    down_across = after(down_across, turned_mats[0])
    down_diagonal = paired(down_across, 1)
    down_mats = [down, down_beside, down_across, down_diagonal]
    fwd_parts = [
        jnp.dot(hidden, mat, preferred_element_type=jnp.float32).astype(jnp.bfloat16)
        for mat in down_mats
    ]

    rows = jnp.concatenate(bwd_blocks)
    gate_value, up_value = rows_times(rows, gate_mats), rows_times(rows, up_mats)
    sigmoid_value = jax.nn.sigmoid(gate_value)
    gate_factor = up_value * sigmoid_value * (1.0 + gate_value * (1.0 - sigmoid_value))
    up_factor = gate_value * sigmoid_value

    landed = lax.optimization_barrier((*grad_blocks[1:], gate_factor, up_factor, *fwd_parts))
    grads = jnp.concatenate([grad_blocks[0], *landed[: experts - 1]])
    quarter = down.shape[1]
    grad_hidden = sum(
        jnp.dot(grads[:, j * quarter : (j + 1) * quarter], mat, preferred_element_type=jnp.float32)
        if j < 2
        else contract_cols(grads[:, j * quarter : (j + 1) * quarter], mat)
        for j, mat in enumerate([down_turned, beside_turned, *down_mats[2:]])
    )
    grad_gate = (grad_hidden * landed[experts - 1]).astype(jnp.bfloat16)
    grad_up = (grad_hidden * landed[experts]).astype(jnp.bfloat16)
    bwd_parts = [
        (
            jnp.dot(grad_gate, g, preferred_element_type=jnp.float32)
            + jnp.dot(grad_up, u, preferred_element_type=jnp.float32)
        ).astype(jnp.bfloat16)
        for g, u in zip(turned_mats[:QUARTERS], turned_mats[QUARTERS:])
    ]
    fwd_parts = landed[experts + 1 :]
    merged = lax.axis_size("pp") == 2

    done = tuple(grad_blocks[1:])
    fwd_meta = jnp.concatenate(
        [fwd_routes[0].reshape(1, tokens).astype(jnp.float32), fwd_gates[0].reshape(1, tokens)]
    )
    bwd_meta = bwd_routes[0].reshape(1, tokens).astype(jnp.float32)
    bwd_meta = jnp.concatenate([bwd_meta, jnp.ones_like(bwd_meta)])

    def returned(parts, steps):
        out = jnp.concatenate(parts, axis=1)
        blocks = [out[d * slot_cap : (d + 1) * slot_cap] for d in range(experts)]
        if experts == 4:
            edge = jnp.where(inner == 1, blocks[0], blocks[3])
            core = jnp.where(inner == 1, blocks[3], blocks[0])
            blocks = [edge, blocks[2], blocks[1], core]
        return [handed(b, steps, d) for b, d in zip(blocks, handed_distances(experts))]

    if merged:
        first = section == 0
        meta = handed(after(jnp.where(first, fwd_meta, bwd_meta), *done), (1, -1), (0, 0))
        parts = [jnp.where(first, fwd, bwd) for fwd, bwd in zip(fwd_parts, bwd_parts)]
        handed_forward, handed_backward = collect(where, meta, returned(parts, (1, -1)), 2)
    else:
        metas = [handed(after(m, *done), (by,), (0, 0)) for m, by in ((fwd_meta, 1), (bwd_meta, -1))]
        (handed_forward,) = collect(where, metas[0], returned(fwd_parts, (1,)), 1)
        (handed_backward,) = collect(where, metas[1], returned(bwd_parts, (-1,)), 1)
    return handed_forward[None], handed_backward[None]


def solution(mesh):
    return jax.shard_map(
        on_device,
        mesh=mesh,
        in_specs=(P("pp", "ep", None),) * 7 + (P("pp", "ep", None, None),) * 3,
        out_specs=(P("pp", "ep", None), P("pp", "ep", None)),
        check_vma=False,
    )
```

```python
import functools

import jax
import jax.numpy as jnp
from jax import lax
from jax.experimental import pallas as pl
from jax.experimental.pallas import tpu as pltpu
from jax.sharding import PartitionSpec as P

QUARTERS = 4


def is_inner(place):
    return (place ^ (place >> 1)) & 1


def sent_distances(experts):
    if experts == 4:
        return ((0, 0), (2, 1), (1, 2), (3, 3))
    return tuple((d, d) for d in range(experts))


def handed_distances(experts):
    if experts == 4:
        return ((3, 0), (2, 1), (1, 2), (0, 3))
    return tuple((d, d) for d in range(experts))


def landed_distances(experts):
    if experts == 4:
        return ((3, 0), (1, 2), (2, 1), (0, 3))
    return tuple((d, d) for d in range(experts))


def expert_at(where_ref, distance):
    outer, inner = distance
    return where_ref[0] ^ (outer + where_ref[3] * (inner - outer))


def target(index, distance):
    return index ^ (QUARTERS * distance[is_inner(index // QUARTERS)])


def after(block, *done):
    return lax.optimization_barrier((block, *done))[0] if done else block


def paired(block, distance, *done):
    block = after(block, *done)
    count = lax.axis_size("ep")
    return lax.ppermute(block, "ep", [(i, i ^ distance) for i in range(count)])


def sent(block, distance, *done):
    block = after(block, *done)
    count = lax.axis_size("ep")
    return lax.ppermute(block, "ep", [(i, target(i, distance)) for i in range(count)])


def handed(block, steps, distance):
    sections, count = lax.axis_size("pp"), lax.axis_size("ep")
    route = [
        (s * count + i, (s + by) * count + target(i, distance))
        for s in range(sections)
        for by in steps
        if 0 <= s + by < sections
        for i in range(count)
    ]
    return lax.ppermute(block, ("pp", "ep"), route)


def slot_matrix(route, expert_of, slot_cap, experts):
    count = route.shape[1]
    named = [route == expert_of(distance) for distance in range(experts)]
    hits = [jnp.where(one, 1.0, 0.0) for one in named]
    hits += [jnp.zeros_like(hits[0])] * (-experts % 8)
    low = lax.broadcasted_iota(jnp.int32, (count, count), 0)
    high = lax.broadcasted_iota(jnp.int32, (count, count), 1)
    earlier = jnp.where(low < high, 1.0, 0.0).astype(jnp.bfloat16)
    place = jnp.dot(
        jnp.concatenate(hits).astype(jnp.bfloat16), earlier, preferred_element_type=jnp.float32
    ).astype(jnp.int32)
    slots = lax.broadcasted_iota(jnp.int32, (slot_cap, count), 0)
    return jnp.concatenate(
        [jnp.where((slots == place[d : d + 1]) & named[d], 1.0, 0.0) for d in range(experts)]
    )


def spread_kernel(slot_cap, experts, where_ref, fwd_ref, bwd_ref, gate_ref, *refs):
    value_refs, out_refs = refs[:3], refs[3:]
    quarter = value_refs[0].shape[1] // QUARTERS
    fwd_slots, bwd_slots = [
        slot_matrix(ref[...], lambda d: expert_at(where_ref, sent_distances(experts)[d]), slot_cap, experts)
        for ref in (fwd_ref, bwd_ref)
    ]
    slot_gate = jnp.sum(bwd_slots * gate_ref[...], axis=1, keepdims=True)
    fwd_slots, bwd_slots = fwd_slots.astype(jnp.bfloat16), bwd_slots.astype(jnp.bfloat16)
    for at, chosen in enumerate((fwd_slots, bwd_slots, bwd_slots)):
        for j in range(QUARTERS):
            start = pl.multiple_of((where_ref[1] ^ j) * quarter, quarter)
            values = value_refs[at][:, pl.ds(start, quarter)]
            rows = jnp.dot(chosen, values, preferred_element_type=jnp.float32)
            if at == 2:
                rows = rows * slot_gate
            for d in range(experts):
                out_refs[at * experts + d][:, j * quarter : (j + 1) * quarter] = rows[
                    d * slot_cap : (d + 1) * slot_cap
                ].astype(jnp.bfloat16)


def spread(where, fwd_routes, bwd_routes, gates, values, slot_cap, experts):
    tokens, width = values[0].shape
    args = [*(row.reshape(1, tokens) for row in (fwd_routes, bwd_routes, gates)), *values]
    out_count = experts * len(values)
    vmem = pl.BlockSpec(memory_space=pltpu.VMEM)
    out = pl.pallas_call(
        functools.partial(spread_kernel, slot_cap, experts),
        in_specs=[pl.BlockSpec(memory_space=pltpu.SMEM)] + [vmem] * len(args),
        out_specs=[vmem] * out_count,
        out_shape=[jax.ShapeDtypeStruct((slot_cap, width), jnp.bfloat16)] * out_count,
        cost_estimate=pl.CostEstimate(
            flops=2 * out_count * slot_cap * tokens * width,
            bytes_accessed=2 * width * (tokens * len(values) + out_count * slot_cap),
            transcendentals=0,
        ),
        compiler_params=pltpu.CompilerParams(vmem_limit_bytes=20 << 20),
    )(where, *[pltpu.with_memory_space_constraint(arg, pltpu.HBM) for arg in args])
    return [out[at * experts : (at + 1) * experts] for at in range(len(values))]


def collect_kernel(slot_cap, experts, where_ref, meta_ref, *refs):
    block_refs, out_refs, (held, stored) = refs[:experts], refs[experts:-2], refs[-2:]
    tokens = meta_ref.shape[1]
    quarter = out_refs[0].shape[1] // QUARTERS
    low = lax.broadcasted_iota(jnp.int32, (tokens, tokens), 1)
    high = lax.broadcasted_iota(jnp.int32, (tokens, tokens), 0)
    route, gate = [
        jnp.sum(jnp.where(low == high, meta_ref[at : at + 1], 0.0), axis=1, keepdims=True)
        for at in range(2)
    ]
    lane = lax.broadcasted_iota(jnp.int32, (1, 128), 1)
    relative = jnp.full((1, 128), -1, jnp.int32)
    for d, distance in enumerate(landed_distances(experts)):
        relative = jnp.where(lane == d, expert_at(where_ref, distance), relative)
    hits = jnp.where(route == relative.astype(jnp.float32), 1.0, 0.0)
    earlier = jnp.where(low < high, 1.0, 0.0).astype(jnp.bfloat16)
    place = jnp.dot(earlier, hits.astype(jnp.bfloat16), preferred_element_type=jnp.float32)
    slots = lax.broadcasted_iota(jnp.int32, (tokens, slot_cap), 1).astype(jnp.float32)
    chosen = jnp.concatenate(
        [
            jnp.where((slots == place[:, d : d + 1]) & (hits[:, d : d + 1] > 0.0), 1.0, 0.0)
            for d in range(experts)
        ],
        axis=1,
    ).astype(jnp.bfloat16)
    copies = []
    for j in range(QUARTERS):
        part = slice(j * quarter, (j + 1) * quarter)
        rows = jnp.concatenate([ref[:, part] for ref in block_refs])
        total = jnp.dot(chosen, rows, preferred_element_type=jnp.float32) * gate
        if len(out_refs) == 1:
            results = [total]
        else:
            first = where_ref[2] == 0
            results = [jnp.where(first, 0.0, total), jnp.where(first, total, 0.0)]
        start = pl.multiple_of((where_ref[1] ^ j) * quarter, quarter)
        for at, result in enumerate(results):
            held[at, j] = result.astype(jnp.bfloat16)
            goal = out_refs[at].at[:, pl.ds(start, quarter)]
            copies.append(pltpu.make_async_copy(held.at[at, j], goal, stored.at[at, j]))
            copies[-1].start()
    for copy in copies:
        copy.wait()


def collect(where, meta, blocks, outputs):
    tokens = meta.shape[1]
    experts = len(blocks)
    slot_cap, width = blocks[0].shape
    quarter = width // QUARTERS
    vmem = pl.BlockSpec(memory_space=pltpu.VMEM)
    return pl.pallas_call(
        functools.partial(collect_kernel, slot_cap, experts),
        in_specs=[pl.BlockSpec(memory_space=pltpu.SMEM)] + [vmem] * (1 + experts),
        out_specs=[pl.BlockSpec(memory_space=pl.ANY)] * outputs,
        scratch_shapes=[
            pltpu.VMEM((outputs, QUARTERS, tokens, quarter), jnp.bfloat16),
            pltpu.SemaphoreType.DMA((outputs, QUARTERS)),
        ],
        out_shape=[jax.ShapeDtypeStruct((tokens, width), jnp.bfloat16)] * outputs,
        cost_estimate=pl.CostEstimate(
            flops=2 * experts * slot_cap * tokens * width,
            bytes_accessed=2 * width * (tokens * outputs + experts * slot_cap),
            transcendentals=0,
        ),
        compiler_params=pltpu.CompilerParams(vmem_limit_bytes=16 << 20),
    )(where, meta, *blocks)


def stage_kernel(*refs):
    count = len(refs) // 2
    arrived = refs[-1]
    copies = [
        pltpu.make_async_copy(refs[at], refs[count + at], arrived.at[at]) for at in range(count)
    ]
    for copy in copies:
        copy.start()
    for copy in copies:
        copy.wait()


def staged(weights):
    count = len(weights)
    return pl.pallas_call(
        stage_kernel,
        in_specs=[pl.BlockSpec(memory_space=pl.ANY)] * count,
        out_specs=[pl.BlockSpec(memory_space=pltpu.VMEM)] * count,
        out_shape=[jax.ShapeDtypeStruct(weight.shape, weight.dtype) for weight in weights],
        scratch_shapes=[pltpu.SemaphoreType.DMA((count,))],
        cost_estimate=pl.CostEstimate(
            flops=0,
            bytes_accessed=sum(2 * weight.size * weight.dtype.itemsize for weight in weights),
            transcendentals=0,
        ),
        compiler_params=pltpu.CompilerParams(vmem_limit_bytes=16 << 20),
    )(*[pltpu.with_memory_space_constraint(weight, pltpu.HBM) for weight in weights])


def turn_kernel(*refs):
    count = len(refs) // 2
    for at in range(count):
        refs[count + at][...] = refs[at][...].T


def turned(mats):
    vmem = pl.BlockSpec(memory_space=pltpu.VMEM)
    return pl.pallas_call(
        turn_kernel,
        in_specs=[vmem] * len(mats),
        out_specs=[vmem] * len(mats),
        out_shape=[jax.ShapeDtypeStruct(mat.shape[::-1], mat.dtype) for mat in mats],
        cost_estimate=pl.CostEstimate(
            flops=0,
            bytes_accessed=sum(2 * mat.size * mat.dtype.itemsize for mat in mats),
            transcendentals=0,
        ),
        compiler_params=pltpu.CompilerParams(vmem_limit_bytes=16 << 20),
    )(*mats)


def rows_times(rows, mats):
    quarter = mats[0].shape[0]
    total = None
    for j, mat in enumerate(mats):
        part = jnp.dot(
            rows[:, j * quarter : (j + 1) * quarter], mat, preferred_element_type=jnp.float32
        )
        total = part if total is None else total + part
    return total


def contract_cols(left, right):
    return lax.dot_general(
        left, right, (((1,), (1,)), ((), ())), preferred_element_type=jnp.float32
    )


def on_device(
    fwd_tokens,
    fwd_routes,
    fwd_gates,
    bwd_tokens,
    bwd_grads,
    bwd_routes,
    bwd_gates,
    gate_proj,
    up_proj,
    down_proj,
):
    experts = lax.axis_size("ep") // QUARTERS
    tokens = fwd_tokens.shape[1]
    slot_cap = 3 * tokens // (2 * experts)
    me = lax.axis_index("ep")
    section = lax.axis_index("pp")
    place = me // QUARTERS
    inner = is_inner(place) if experts == 4 else jnp.zeros_like(place)
    where = jnp.stack([place, me % QUARTERS, section, inner]).astype(jnp.int32)

    gate, up, down = gate_proj[0, 0], up_proj[0, 0], down_proj[0, 0]
    gate_across = paired(gate, 2)
    up_across = paired(up, 2)
    gate_beside = paired(gate, 1)
    up_beside = paired(up, 1)
    down_beside = paired(down, 1)
    fwd_spread, row_spread, grad_spread = spread(
        after(where, gate_beside),
        fwd_routes[0],
        bwd_routes[0],
        bwd_gates[0],
        (fwd_tokens[0], bwd_tokens[0], bwd_grads[0]),
        slot_cap,
        experts,
    )
    order = sorted(range(1, experts), reverse=True)
    distances = sent_distances(experts)
    last = order[-1]
    fwd_blocks, bwd_blocks, grad_blocks = {}, {}, {}
    for d in order:
        before = (up_beside, down_beside) if d == last else ()
        fwd_blocks[d] = sent(fwd_spread[d], distances[d], *before)
    for d in order:
        bwd_blocks[d] = sent(row_spread[d], distances[d], fwd_blocks[d])
    down_across = paired(down, 2, gate_across)
    gate_diagonal = paired(gate_across, 1, bwd_blocks[last])
    up_diagonal = paired(up_across, 1, bwd_blocks[last])
    for d in order:
        before = ()
        grad_blocks[d] = sent(grad_spread[d], distances[d], bwd_blocks[d], *before)
    near = lax.optimization_barrier((gate_across, down_beside, fwd_blocks[last]))
    gate_across, down_beside = staged(near[:2])
    near = lax.optimization_barrier((up_across, bwd_blocks[last]))
    (up_across,) = staged(near[:1])
    gate_mats = [gate, gate_beside, gate_across, gate_diagonal]
    up_mats = [up, up_beside, up_across, up_diagonal]
    fwd_blocks = [fwd_spread[0]] + [fwd_blocks[d] for d in range(1, experts)]
    bwd_blocks = [row_spread[0]] + [bwd_blocks[d] for d in range(1, experts)]
    grad_blocks = [grad_spread[0]] + [grad_blocks[d] for d in range(1, experts)]

    rows = jnp.concatenate(fwd_blocks)
    gate_value, up_value = rows_times(rows, gate_mats), rows_times(rows, up_mats)
    hidden = (jax.nn.silu(gate_value) * up_value).astype(jnp.bfloat16)
    ready = lax.optimization_barrier((*gate_mats, *up_mats, down, down_beside, hidden))[:-1]
    *turned_mats, down_turned, beside_turned = turned(ready)
    down_across = after(down_across, turned_mats[0])
    down_diagonal = paired(down_across, 1)
    down_mats = [down, down_beside, down_across, down_diagonal]
    fwd_parts = [
        jnp.dot(hidden, mat, preferred_element_type=jnp.float32).astype(jnp.bfloat16)
        for mat in down_mats
    ]

    rows = jnp.concatenate(bwd_blocks)
    gate_value, up_value = rows_times(rows, gate_mats), rows_times(rows, up_mats)
    sigmoid_value = jax.nn.sigmoid(gate_value)
    gate_factor = up_value * sigmoid_value * (1.0 + gate_value * (1.0 - sigmoid_value))
    up_factor = gate_value * sigmoid_value

    late_turned = turned(down_mats[2:])
    landed = lax.optimization_barrier(
        (*grad_blocks[1:], gate_factor, up_factor, *fwd_parts, *late_turned)
    )
    grads = jnp.concatenate([grad_blocks[0], *landed[: experts - 1]])
    quarter = down.shape[1]
    grad_hidden = sum(
        jnp.dot(grads[:, j * quarter : (j + 1) * quarter], mat, preferred_element_type=jnp.float32)
        for j, mat in enumerate([down_turned, beside_turned, *landed[-2:]])
    )
    grad_gate = (grad_hidden * landed[experts - 1]).astype(jnp.bfloat16)
    grad_up = (grad_hidden * landed[experts]).astype(jnp.bfloat16)
    bwd_parts = [
        (
            jnp.dot(grad_gate, g, preferred_element_type=jnp.float32)
            + jnp.dot(grad_up, u, preferred_element_type=jnp.float32)
        ).astype(jnp.bfloat16)
        for g, u in zip(turned_mats[:QUARTERS], turned_mats[QUARTERS:])
    ]
    fwd_parts = landed[experts + 1 : -2]
    merged = lax.axis_size("pp") == 2

    done = tuple(grad_blocks[1:])
    fwd_meta = jnp.concatenate(
        [fwd_routes[0].reshape(1, tokens).astype(jnp.float32), fwd_gates[0].reshape(1, tokens)]
    )
    bwd_meta = bwd_routes[0].reshape(1, tokens).astype(jnp.float32)
    bwd_meta = jnp.concatenate([bwd_meta, jnp.ones_like(bwd_meta)])

    def returned(parts, steps):
        out = jnp.concatenate(parts, axis=1)
        blocks = [out[d * slot_cap : (d + 1) * slot_cap] for d in range(experts)]
        if experts == 4:
            edge = jnp.where(inner == 1, blocks[0], blocks[3])
            core = jnp.where(inner == 1, blocks[3], blocks[0])
            blocks = [edge, blocks[2], blocks[1], core]
        return [handed(b, steps, d) for b, d in zip(blocks, handed_distances(experts))]

    if merged:
        first = section == 0
        meta = handed(after(jnp.where(first, fwd_meta, bwd_meta), *done), (1, -1), (0, 0))
        parts = [jnp.where(first, fwd, bwd) for fwd, bwd in zip(fwd_parts, bwd_parts)]
        handed_forward, handed_backward = collect(where, meta, returned(parts, (1, -1)), 2)
    else:
        metas = [handed(after(m, *done), (by,), (0, 0)) for m, by in ((fwd_meta, 1), (bwd_meta, -1))]
        (handed_forward,) = collect(where, metas[0], returned(fwd_parts, (1,)), 1)
        (handed_backward,) = collect(where, metas[1], returned(bwd_parts, (-1,)), 1)
    return handed_forward[None], handed_backward[None]


def solution(mesh):
    return jax.shard_map(
        on_device,
        mesh=mesh,
        in_specs=(P("pp", "ep", None),) * 7 + (P("pp", "ep", None, None),) * 3,
        out_specs=(P("pp", "ep", None), P("pp", "ep", None)),
        check_vma=False,
    )
```
